32 devices in a mesh: member: 2 (over x), horiz: 4 (over y, core), vert: 4 (over z).
Axes of the slice: x: 2, y: 2, z: 4, core: 2. Of those that a mesh axis runs over, the one named last changes fastest.
Arguments:
- velocity: float32 [6, 64, 288, 128], P('member', 'horiz', 'vert'), parts along dimension 0, may hold values from -6 to 6
- stress: float32 [12, 64, 288, 128], P('member', 'horiz', 'vert'), parts along dimension 0, may hold values from -6 to 6
- material_index: int32 [288], P('vert'), may hold values from 0 to 7
- material_table: float32 [8, 4], replicated, may hold values from 0.5 to 1.5
- split_level: int32 [1], replicated, may hold values from 72 to 143
- source_x: int32 [16], replicated, may hold values from 0 to 63
- source_z: int32 [16], replicated, may hold values from 0 to 287
- source_y: int32 [16], replicated, may hold values from 0 to 127
- amplitude: float32 [32], P('member'), parts along dimension 0, may hold values from 1 to 10
Outputs:
- velocity_out: float32 [6, 64, 288, 128], P('member', 'horiz', 'vert'), parts along dimension 0
- stress_out: float32 [12, 64, 288, 128], P('member', 'horiz', 'vert'), parts along dimension 0
The draws below stay inside these ranges and needn't reach their ends.
There are 2 independent parts, one for each index of `member`. The reference program is written for one: setup_inputs(seed, part) draws one part's arguments, and reference() takes and returns one part's arrays. A program takes and returns all parts, laid end to end along the dimension named above; an argument that names none is the same for every part. Nothing has to cross between parts.
All inputs are finite; a program needn't handle non-finite values.
Results may differ from the reference program's by a relative error of at most 0.000082.
Values sent between devices are 32-bit elements; how exact they have to be, the bound alone decides.
No kernel may reach another device: no remote copies, remote signals or barrier semaphores. Data moves between devices by JAX's collectives and lax.ppermute only.
A program may use at most 64 MiB of HBM per device.

```python
import math
import jax
import jax.numpy as jnp
from jax import lax

NSRC = 16
NMAT = 8
NX = 64
NZ = 288
NY = 128


def touch_ends(drawn, key, smallest, high):
    extent = drawn.shape
    index_at = [jax.random.randint(jax.random.fold_in(key, axis), (), 0, extent[axis]) for axis in range(len(extent))]
    drawn = drawn.at[tuple(index_at)].set(smallest)
    longest = extent.index(max(extent))
    index_at[longest] = (index_at[longest] + 1) % extent[longest]
    return drawn.at[tuple(index_at)].set(high)


def shard_levels(rng, extent, pieces, least, top_value):
    gain = 1.0
    for dim, blocks in pieces:
        steps = jax.random.uniform(jax.random.fold_in(jax.random.fold_in(rng, 6), dim), (blocks,), jnp.float32, least / len(pieces), top_value / len(pieces))
        gain = gain * jnp.repeat(jnp.exp(steps), extent[dim] // blocks).reshape((-1,) + (1,) * (len(extent) - 1 - dim))
    return gain


def noise(stream_key, shape, deviation, limit, pieces=(), kind=jnp.bfloat16):
    entries = deviation * jax.random.normal(stream_key, shape, jnp.float32)
    if pieces:
        entries = entries * shard_levels(stream_key, shape, pieces, -0.22, 0.18)
    return jnp.clip(entries, -limit, limit).astype(kind)


def setup_inputs(seed: int = 0, part: int = 0) -> dict:
    splits = jax.random.split(jax.random.key(seed), 10)
    own_keys = jax.random.split(jax.random.fold_in(splits[9], part), 10)
    velocity = noise(own_keys[0], (3, NX, NZ, NY), 1.0, 6.0, ((1, 4), (2, 4)), jnp.float32)
    stress = noise(own_keys[1], (6, NX, NZ, NY), 1.0, 6.0, ((1, 4), (2, 4)), jnp.float32)
    material_index = touch_ends(jax.random.randint(splits[2], (NZ,), 0, NMAT), jax.random.fold_in(splits[2], 1), 0, NMAT - 1).astype(jnp.int32)
    material_table = jnp.clip(jax.random.uniform(splits[3], (NMAT, 4), jnp.float32, 0.5, 1.5), 0.5, 1.5)
    split_level = jax.random.randint(splits[4], (1,), NZ // 4, NZ // 2).astype(jnp.int32)
    source_x = touch_ends(jax.random.randint(splits[5], (NSRC,), 0, NX), jax.random.fold_in(splits[5], 1), 0, NX - 1).astype(jnp.int32)
    source_z = touch_ends(jax.random.randint(splits[6], (NSRC,), 0, NZ), jax.random.fold_in(splits[6], 1), 0, NZ - 1).astype(jnp.int32)
    source_y = touch_ends(jax.random.randint(splits[7], (NSRC,), 0, NY), jax.random.fold_in(splits[7], 1), 0, NY - 1).astype(jnp.int32)
    amplitude = jnp.clip(jnp.exp(jax.random.uniform(own_keys[8], (NSRC,), jnp.float32, math.log(1.0), math.log(10.0))), 1.0, 10.0)
    return dict(velocity=velocity, stress=stress, material_index=material_index, material_table=material_table, split_level=split_level, source_x=source_x, source_z=source_z, source_y=source_y, amplitude=amplitude)


courant = 0.2
wavelet = (1.0, -0.5)
pair_table = ((0, 3, 4), (3, 1, 5), (4, 5, 2))


def zero_rim(field, axis):
    return jnp.zeros_like(lax.slice_in_dim(field, 0, 1, axis=axis))


def backward(field, axis, edge):
    if edge is None:
        edge = zero_rim(field, axis)
    count = field.shape[axis]
    before = jnp.concatenate([edge, lax.slice_in_dim(field, 0, count - 1, axis=axis)], axis)
    return field - before


def forward(field, axis, edge):
    if edge is None:
        edge = zero_rim(field, axis)
    count = field.shape[axis]
    after = jnp.concatenate([lax.slice_in_dim(field, 1, count, axis=axis), edge], axis)
    return after - field


def velocity_update(speeds, forces, coeff, chooser):
    result = []
    for k in range(3):
        total = backward(forces[pair_table[k][0]], 0, chooser(k, 0))
        total = total + backward(forces[pair_table[k][1]], 1, chooser(k, 1))
        total = total + backward(forces[pair_table[k][2]], 2, chooser(k, 2))
        result.append((1.0 - courant * coeff[3]) * speeds[k] + courant * coeff[0] * total)
    return result


def stress_update(speeds, forces, coeff, chooser, source, wave):
    grads = [[forward(speeds[i], j, chooser(i, j)) for j in range(3)] for i in range(3)]
    spread = grads[0][0] + grads[1][1] + grads[2][2]
    result = []
    for c in range(3):
        result.append(forces[c] + courant * (coeff[1] * spread + 2.0 * coeff[2] * grads[c][c]) + courant * wave * source)
    for i, j in ((0, 1), (0, 2), (1, 2)):
        result.append(forces[pair_table[i][j]] + courant * coeff[2] * (grads[i][j] + grads[j][i]))
    return result


def no_edge(k, axis):
    return None


def reference(velocity, stress, material_index, material_table, split_level, source_x, source_z, source_y, amplitude):
    table = material_table[material_index]
    levels = jnp.arange(NZ, dtype=jnp.int32)
    solid = (levels >= split_level[0]).astype(jnp.float32)
    columns = [table[:, 0], table[:, 1], table[:, 2] * solid, table[:, 3]]
    coeff = [column[None, :, None] for column in columns]
    source = jnp.zeros((NX, NZ, NY), jnp.float32).at[source_x, source_z, source_y].add(amplitude)
    speeds = [velocity[k] for k in range(3)]
    forces = [stress[c] for c in range(6)]
    for step in range(2):
        speeds = velocity_update(speeds, forces, coeff, no_edge)
        forces = stress_update(speeds, forces, coeff, no_edge, source, wavelet[step])
    return jnp.stack(speeds), jnp.stack(forces)
```

```python
import functools

import jax
import jax.numpy as jnp
from jax import lax
from jax.experimental import pallas as pl
from jax.experimental.pallas import tpu as pltpu
from jax.sharding import PartitionSpec as P

courant = 0.2
wavelet = (1.0, -0.5)
pair_table = ((0, 3, 4), (3, 1, 5), (4, 5, 2))
front = (0, 3, 4)
top = (3, 1, 5)
PAD = 8
ANY = pl.BlockSpec(memory_space=pl.ANY)
VMEM = pl.BlockSpec(memory_space=pltpu.VMEM)
SMEM = pl.BlockSpec(memory_space=pltpu.SMEM)


def swap_pairs(rows, cols, along, odd):
    out = []
    for i in range(rows):
        for j in range(cols):
            at, size = (i, rows) if along == 0 else (j, cols)
            if not odd:
                to = at ^ 1
            elif at in (0, size - 1):
                to = None
            else:
                to = at + 1 if at % 2 else at - 1
            if along == 0:
                target = (i, j ^ 1) if to is None else (to, j)
            else:
                target = (i ^ 1, j) if to is None else (i, to)
            out.append((i * cols + j, target[0] * cols + target[1]))
    return out


def swap(block, along, odd):
    rows, cols = lax.axis_size("horiz"), lax.axis_size("vert")
    return lax.ppermute(block, ("horiz", "vert"), swap_pairs(rows, cols, along, odd))


def lane_of(shape):
    return lax.broadcasted_iota(jnp.int32, shape, len(shape) - 1)


def back_lane(a):
    moved = pltpu.roll(a, 1, 1)
    return a - jnp.where(lane_of(a.shape) == 0, 0.0, moved)


def fore_lane(a):
    last = a.shape[-1] - 1
    moved = pltpu.roll(a, last, 1)
    return jnp.where(lane_of(a.shape) == last, 0.0, moved) - a


def velocity_tile(s_at, v_at, rb, dq):
    out = []
    for k in range(3):
        a, b, c = pair_table[k]
        total = (s_at(a, 0, 0) - s_at(a, -1, 0)) + (s_at(b, 0, 0) - s_at(b, 0, -1))
        total = total + back_lane(s_at(c, 0, 0))
        out.append(dq * v_at(k) + rb * total)
    return out


def strain(v_at):
    grads = []
    for i in range(3):
        here = v_at(i, 0, 0)
        grads.append([v_at(i, 1, 0) - here, v_at(i, 0, 1) - here, fore_lane(here)])
    return grads


def stress_terms(g, rl, rm, wanted=range(6)):
    out = {}
    if any(c < 3 for c in wanted):
        spread = rl * (g[0][0] + g[1][1] + g[2][2])
    for c in wanted:
        if c < 3:
            out[c] = spread + 2.0 * rm * g[c][c]
        else:
            i, j = ((0, 1), (0, 2), (1, 2))[c - 3]
            out[c] = rm * (g[i][j] + g[j][i])
    return out


def memo(fn):
    seen = {}

    def call(*key):
        if key not in seen:
            seen[key] = fn(*key)
        return seen[key]

    return call


MSG = 200


def level_scalars(index_ref, table_ref, split_ref, z, offset):
    kind = index_ref[z]
    solid = jnp.where(offset + z >= split_ref[0], 1.0, 0.0)
    return (
        courant * table_ref[kind, 0],
        1.0 - courant * table_ref[kind, 3],
        courant * table_ref[kind, 1],
        courant * (table_ref[kind, 2] * solid),
    )


def edge_kernel(n, m, y, v_ref, s_ref, index_ref, table_ref, split_ref, out_a, out_b, low, high, sems):
    vert = lax.axis_index("vert")
    odd = vert % 2 == 1
    copies = []
    for at, (buf, start) in enumerate(((low, 0), (high, m - 8))):
        copies.append(
            pltpu.make_async_copy(s_ref.at[:, :, pl.ds(start, 8), :], buf.at[pl.ds(0, 6), pl.ds(1, n)], sems.at[2 * at])
        )
        copies.append(
            pltpu.make_async_copy(
                v_ref.at[:, :, pl.ds(start, 8), :], buf.at[pl.ds(6, 3), pl.ds(1, n)], sems.at[2 * at + 1]
            )
        )
    for copy in copies:
        copy.start()
    for buf in (low, high):
        for f in front:
            buf[f, 0] = jnp.zeros((8, y), jnp.float32)
    offset = vert * m
    at_first = level_scalars(index_ref, table_ref, split_ref, 0, offset)
    at_second = level_scalars(index_ref, table_ref, split_ref, 1, offset)
    at_last = level_scalars(index_ref, table_ref, split_ref, m - 1, offset)
    for copy in copies:
        copy.wait()
    low2 = low.reshape(9 * (n + 1) * 8, y)
    high2 = high.reshape(9 * (n + 1) * 8, y)

    def row(buf, f, z, dx=0):
        return buf[pl.Slice((f * (n + 1) + 1 + dx) * 8 + z, n, 8), :]

    def moved(buf, z, scal):
        return velocity_tile(
            memo(lambda f, dx, dz: row(buf, f, z + dz, dx)), lambda k: row(buf, 6 + k, z), scal[0], scal[1]
        )

    up = [row(high2, f, 7) for f in range(6)] + moved(high2, 7, at_last)
    down = [row(low2, f, 0) for f in range(9)] + moved(low2, 1, at_second)

    def put(at, rows, up_value, down_value):
        out_a[pl.ds(at, rows), :] = jnp.where(odd, down_value, up_value)
        out_b[pl.ds(at, rows), :] = jnp.where(odd, up_value, down_value)

    for f in range(12):
        put(f * n, n, up[f] if f < 9 else down[f], down[f])
    base = 12 * n
    for c in range(4):
        splat = [jnp.full((1, y), a[c], jnp.float32) for a in (at_last, at_first)]
        put(base + c, 1, *splat)
    ahead = jnp.full((1, y), at_second[0], jnp.float32)
    put(base + 4, 1, ahead, ahead)
    for c, f in enumerate(front):
        corner = low[f, n, pl.ds(1, 1), :]
        put(base + 5 + c, 1, corner, corner)


def level_kernel(m, index_ref, table_ref, split_ref, out_ref):
    offset = lax.axis_index("vert") * m
    y = out_ref.shape[-1]

    def body(z, carry):
        for c, value in enumerate(level_scalars(index_ref, table_ref, split_ref, z, offset)):
            out_ref[c, pl.ds(z, 1), :] = jnp.full((1, y), value, jnp.float32)
        return carry

    lax.fori_loop(0, m, body, 0, unroll=8)


def sort_levels(a_ref, b_ref, below, above):
    vert = lax.axis_index("vert")
    odd = vert % 2 == 1
    has_below = jnp.where(vert > 0, 1.0, 0.0)
    has_above = jnp.where(vert < lax.axis_size("vert") - 1, 1.0, 0.0)
    for t in range(MSG // 8):
        at = pl.ds(8 * t, 8)
        a, b = a_ref[at, :], b_ref[at, :]
        below[at, :] = has_below * jnp.where(odd, a, b)
        above[at, :] = has_above * jnp.where(odd, b, a)


def add_sources(add_row, plane_x, z_low, z_high, scale, x_at, z_at, src):
    sx, sz, sy, amp = src

    def body(i, carry):
        z = sz[i] - z_at

        @pl.when((sx[i] - x_at == plane_x) & (z >= z_low) & (z < z_high))
        def _():
            lane = lane_of((1, 128))
            add_row(z, jnp.where(lane == sy[i], scale * amp[i], 0.0))

        return carry

    lax.fori_loop(0, sx.shape[0], body, 0)


def plane_kernel(
    n, m, y, v_ref, s_ref, a_ref, b_ref, level_ref, sx, sz, sy, amp,
    out_a, out_b, coef, below, above, sl, vl, sr, vr, msg, sems,
):
    horiz, vert = lax.axis_index("horiz"), lax.axis_index("vert")
    body = pl.ds(PAD, m)
    copies = [
        pltpu.make_async_copy(s_ref.at[:, pl.ds(0, 2)], sl.at[:, pl.ds(1, 2), body], sems.at[0]),
        pltpu.make_async_copy(v_ref.at[:, pl.ds(0, 2)], vl.at[:, :, body], sems.at[1]),
        pltpu.make_async_copy(s_ref.at[:, pl.ds(n - 2, 2)], sr.at[:, :, body], sems.at[2]),
        pltpu.make_async_copy(v_ref.at[:, pl.ds(n - 1, 1)], vr.at[:, pl.ds(0, 1), body], sems.at[3]),
    ]
    for copy in copies:
        copy.start()
    sort_levels(a_ref, b_ref, below, above)
    lowest, first, second = PAD - 1, PAD + m, PAD + m + 1
    base = 12 * n
    for c in range(4):
        coef[c, body, :] = level_ref[c]
        coef[c, pl.ds(lowest, 1), :] = below[pl.ds(base + c, 1), :]
        coef[c, pl.ds(first, 1), :] = above[pl.ds(base + c, 1), :]
    coef[0, pl.ds(second, 1), :] = above[pl.ds(base + 4, 1), :]
    for f in front:
        sl[f, 0] = jnp.zeros((m + 16, y), jnp.float32)
    for k in range(3):
        vr[k, 1] = jnp.zeros((m + 16, y), jnp.float32)

    for x, buf, at in ((0, sl, 1), (1, sl, 2), (n - 2, sr, 0), (n - 1, sr, 1)):
        for f in range(6):
            buf[f, at, pl.ds(lowest, 1), :] = below[pl.ds(f * n + x, 1), :]
            buf[f, at, pl.ds(first, 1), :] = above[pl.ds(f * n + x, 1), :]
    for x, buf, at in ((0, vl, 0), (1, vl, 1), (n - 1, vr, 0)):
        for k in range(3):
            buf[k, at, pl.ds(lowest, 1), :] = below[pl.ds((6 + k) * n + x, 1), :]
            buf[k, at, pl.ds(first, 1), :] = above[pl.ds((6 + k) * n + x, 1), :]
            buf[k, at, pl.ds(second, 1), :] = above[pl.ds((9 + k) * n + x, 1), :]

    tiles = [(PAD + 8 * t, 8) for t in range(m // 8)]
    right, left = horiz % 2, 1 - horiz % 2
    tail = 6 * m

    def cs(c, r, size):
        return coef[c, pl.ds(r, size), :]

    def move(s_buf, v_buf, s_at, v_at, r, size):
        new = velocity_tile(
            memo(lambda f, dx, dz: s_buf[f, s_at + dx, pl.ds(r + dz, size), :]),
            lambda k: v_buf[k, v_at, pl.ds(r, size), :],
            cs(0, r, size),
            cs(1, r, size),
        )
        for k in range(3):
            v_buf[k, v_at, pl.ds(r, size), :] = new[k]
        return new

    def load(s_buf, v_buf, s_at, v_at, r, size, wanted):
        g = strain(memo(lambda k, dx, dz: v_buf[k, v_at + dx, pl.ds(r + dz, size), :]))
        terms = stress_terms(g, cs(2, r, size), cs(3, r, size), wanted)
        for c in wanted:
            s_buf[c, s_at, pl.ds(r, size), :] = s_buf[c, s_at, pl.ds(r, size), :] + terms[c]

    copies[2].wait()
    copies[3].wait()
    for c, f in enumerate(front):
        for r, size in tiles:
            msg[right, pl.ds(c * m + r - PAD, size), :] = sr[f, 1, pl.ds(r, size), :]
        msg[right, pl.ds(tail + c, 1), :] = sr[f, 1, pl.ds(lowest, 1), :]
        msg[right, pl.ds(tail + 3 + c, 1), :] = sr[f, 1, pl.ds(first, 1), :]
        msg[right, pl.ds(tail + 6 + c, 1), :] = above[pl.ds(base + 5 + c, 1), :]
    for r, size in tiles + [(first, 1)]:
        move(sr, vr, 1, 0, r, size)
    for r, size in tiles + [(first, 1)]:
        load(sr, vr, 1, 0, r, size, front)

    x_at, z_at = horiz * n, vert * m
    src = (sx, sz, sy, amp)
    scale = courant * wavelet[0]

    def add_right(z, row):
        at = pl.ds(PAD + z, 1)
        sr[0, 1, at, :] = sr[0, 1, at, :] + row

    add_sources(add_right, n - 1, 0, m + 1, scale, x_at, z_at, src)
    for c, f in enumerate(front):
        for r, size in tiles:
            msg[right, pl.ds((3 + c) * m + r - PAD, size), :] = sr[f, 1, pl.ds(r, size), :]
        msg[right, pl.ds(tail + 9 + c, 1), :] = sr[f, 1, pl.ds(first, 1), :]

    copies[0].wait()
    copies[1].wait()
    for r, size in tiles + [(first, 1)]:
        new = move(sl, vl, 1, 0, r, size)
        for k in range(3):
            at = k * m + r - PAD if r < first else tail + 3 + k
            msg[left, pl.ds(at, size), :] = new[k]
        move(sl, vl, 2, 1, r, size)
    for k in range(3):
        msg[left, pl.ds(tail + k, 1), :] = vl[k, 0, pl.ds(lowest, 1), :]
    load(sl, vl, 1, 0, lowest, 1, top)
    for r, size in tiles:
        load(sl, vl, 1, 0, r, size, range(6))

    def add_left(z, row):
        at = pl.ds(PAD + z, 1)
        for c in range(3):
            sl[c, 1, at, :] = sl[c, 1, at, :] + row

    add_sources(add_left, 0, -1, m, scale, x_at, z_at, src)
    for r, size in tiles:
        new = move(sl, vl, 1, 0, r, size)
        for k in range(3):
            msg[left, pl.ds((3 + k) * m + r - PAD, size), :] = new[k]
    done = [
        pltpu.make_async_copy(msg.at[0], out_a, sems.at[0]),
        pltpu.make_async_copy(msg.at[1], out_b, sems.at[1]),
    ]
    for copy in done:
        copy.start()
    for copy in done:
        copy.wait()


def main_kernel(
    n, m, y, v_ref, s_ref, a_ref, b_ref, coef, sx, sz, sy, amp,
    out_v, out_s, below, above, sb, vb, count, in_v, in_s, off_v, off_s,
):
    horiz, vert = lax.axis_index("horiz"), lax.axis_index("vert")
    body = pl.ds(PAD, m)
    x_at, z_at = horiz * n, vert * m

    def v_in(x):
        return pltpu.make_async_copy(v_ref.at[:, x], vb.at[:, x, body], in_v.at[x])

    def s_in(x):
        return pltpu.make_async_copy(s_ref.at[:, x], sb.at[:, x + 1, body], in_s.at[x])

    def v_off(x):
        return pltpu.make_async_copy(vb.at[:, x, body], out_v.at[:, x], off_v.at[x])

    def s_off(x):
        return pltpu.make_async_copy(sb.at[:, x + 1, body], out_s.at[:, x], off_s.at[x])

    def begin(x, carry):
        s_in(x).start()
        v_in(x).start()
        count[x] = 0
        return carry

    lax.fori_loop(0, n, begin, 0)

    def tally(i, carry):
        x, z = sx[i] - x_at, sz[i] - z_at

        @pl.when((x >= 0) & (x < n) & (z >= -1) & (z <= m))
        def _():
            count[x] = count[x] + 1

        return carry

    lax.fori_loop(0, sx.shape[0], tally, 0)
    sort_levels(a_ref, b_ref, below, above)
    lowest, first, second = PAD - 1, PAD + m, PAD + m + 1
    for f in front:
        sb[f, 0] = jnp.zeros((m + 16, y), jnp.float32)
    for k in range(3):
        vb[k, n] = jnp.zeros((m + 16, y), jnp.float32)
    high = m + 16
    s2 = sb.reshape(6 * (n + 1) * high, y)
    v2 = vb.reshape(3 * (n + 1) * high, y)
    for f in range(6):
        start = (f * (n + 1) + 1) * high
        s2[pl.Slice(start + lowest, n, high), :] = below[pl.ds(f * n, n), :]
        s2[pl.Slice(start + first, n, high), :] = above[pl.ds(f * n, n), :]
    for k in range(3):
        start = k * (n + 1) * high
        v2[pl.Slice(start + lowest, n, high), :] = below[pl.ds((6 + k) * n, n), :]
        v2[pl.Slice(start + first, n, high), :] = above[pl.ds((6 + k) * n, n), :]
        v2[pl.Slice(start + second, n, high), :] = above[pl.ds((9 + k) * n, n), :]

    tiles = [(PAD + 8 * t, 8) for t in range(m // 8)]

    def cs(c, r, size):
        return coef[c, pl.ds(r, size), :]

    def move(x):
        for r, size in tiles + [(first, 1)]:
            new = velocity_tile(
                memo(lambda f, dx, dz: sb[f, x + 1 + dx, pl.ds(r + dz, size), :]),
                lambda k: vb[k, x, pl.ds(r, size), :],
                cs(0, r, size),
                cs(1, r, size),
            )
            for k in range(3):
                vb[k, x, pl.ds(r, size), :] = new[k]

    def load(x, step):
        parts = [(r, size, range(6)) for r, size in tiles]
        if step == 0:
            parts += [(lowest, 1, top), (first, 1, range(6))]
        for r, size, wanted in parts:
            g = strain(memo(lambda k, dx, dz: vb[k, x + dx, pl.ds(r + dz, size), :]))
            terms = stress_terms(g, cs(2, r, size), cs(3, r, size), wanted)
            for c in wanted:
                sb[c, x + 1, pl.ds(r, size), :] = sb[c, x + 1, pl.ds(r, size), :] + terms[c]

        def add(z, row):
            at = pl.ds(PAD + z, 1)
            for c in range(3):
                sb[c, x + 1, at, :] = sb[c, x + 1, at, :] + row

        @pl.when(count[x] > 0)
        def _():
            span = (-1, m + 1) if step == 0 else (0, m)
            add_sources(add, x, *span, courant * wavelet[step], x_at, z_at, (sx, sz, sy, amp))

    def advance(i, carry):
        @pl.when(i < n)
        def _():
            s_in(i).wait()
            v_in(i).wait()
            move(i)

        @pl.when((i >= 1) & (i <= n))
        def _():
            load(i - 1, 0)
            move(i - 1)
            v_off(i - 1).start()

        @pl.when(i >= 2)
        def _():
            load(i - 2, 1)
            s_off(i - 2).start()

        return carry

    lax.fori_loop(0, n + 2, advance, 0)

    def finish(x, carry):
        v_off(x).wait()
        s_off(x).wait()
        return carry

    lax.fori_loop(0, n, finish, 0)


def join_kernel(
    n, m, y, ra, rb_, ma, mb, coef, v_in, s_in, v_out, s_out,
    held, ea, wa, da, ds, dv, dw, qb, db, es, ev, vn, v0, v1, s0, s1, sems,
):
    horiz = lax.axis_index("horiz")
    copies = [pltpu.make_async_copy(src, held.at[i], sems.at[i]) for i, src in enumerate((ra, rb_, ma, mb))]
    planes = [
        (v_in.at[:, pl.ds(0, 2)], v_out.at[:, pl.ds(0, 2)], v0),
        (v_in.at[:, pl.ds(n - 1, 1)], v_out.at[:, pl.ds(n - 1, 1)], v1),
        (s_in.at[:, pl.ds(0, 2)], s_out.at[:, pl.ds(0, 2)], s0),
        (s_in.at[:, pl.ds(n - 2, 2)], s_out.at[:, pl.ds(n - 2, 2)], s1),
    ]
    fetch = [pltpu.make_async_copy(src, buf, sems.at[4 + i]) for i, (src, _, buf) in enumerate(planes)]
    store = [pltpu.make_async_copy(buf, dst, sems.at[4 + i]) for i, (_, dst, buf) in enumerate(planes)]
    for copy in copies + fetch:
        copy.start()
    right, left = horiz % 2, 1 - horiz % 2
    has_left = jnp.where(horiz > 0, 1.0, 0.0)
    has_right = jnp.where(horiz < lax.axis_size("horiz") - 1, 1.0, 0.0)
    lowest, first, second = PAD - 1, PAD + m, PAD + m + 1
    tail = 6 * m
    tiles = [(PAD + 8 * t, 8) for t in range(m // 8)]

    def cs(c, r, size):
        return coef[c, pl.ds(r, size), :]

    def msg(which, c, r, size):
        return held[which, pl.ds(c * m + r - PAD, size), :]

    def end(which, at):
        return held[which, pl.ds(tail + at, 1), :]

    for copy in copies:
        copy.wait()

    for k in range(3):
        rows = [(r, size, msg(left, k, r, size)) for r, size in tiles]
        rows += [(r, 1, end(left, at + k)) for r, at in ((lowest, 0), (first, 3), (second, 6))]
        for r, size, value in rows:
            da[k, pl.ds(r, size), :] = -(has_left * cs(0, r, size)) * value
        rows = [(r, size, msg(left, 3 + k, r, size), msg(2 + left, k, r, size)) for r, size in tiles]
        rows += [(first, 1, end(left, 9 + k), end(2 + left, 3 + k))]
        for r, size, value, own in rows:
            gain = cs(3, r, size) if k else cs(2, r, size) + 2.0 * cs(3, r, size)
            wa[k, pl.ds(r, size), :] = has_left * (value + gain * (own + da[k, pl.ds(r, size), :]))
        rows = [(r, size, msg(2 + right, k, r, size), msg(right, k, r, size)) for r, size in tiles]
        rows += [(r, 1, end(2 + right, at + k), end(right, at + k)) for r, at in ((lowest, 0), (first, 3))]
        for r, size, value, other in rows:
            change = -(has_right * cs(0, r, size)) * value
            db[k, pl.ds(r, size), :] = change
            qb[k, pl.ds(r, size), :] = has_right * other + change

    def flat(buf):
        def at(k, dx, dz, r, size):
            if dx:
                return None
            return buf[k, pl.ds(r + dz, size), :]

        return at

    def strain_of(buf, r, size, ahead=None):
        grads = []
        for i in range(3):
            here = buf[i, pl.ds(r, size), :]
            beyond = -here if ahead is None else ahead[i, pl.ds(r, size), :] - here
            grads.append([beyond, buf[i, pl.ds(r + 1, size), :] - here, fore_lane(here)])
        return grads

    for out, src, ends in ((ds, da, (lowest, first)), (es, db, (lowest,))):
        parts = [(r, size, range(6)) for r, size in tiles]
        parts += [(r, 1, top if r == lowest else range(6)) for r in ends]
        for r, size, wanted in parts:
            terms = stress_terms(strain_of(src, r, size), cs(2, r, size), cs(3, r, size), wanted)
            for c in wanted:
                out[c, pl.ds(r, size), :] = terms[c]

    for r, size in tiles + [(first, 1)]:
        rb, dq = cs(0, r, size), cs(1, r, size)
        for k in range(3):
            a, b, c = pair_table[k]
            here = ds[a, pl.ds(r, size), :]
            total = here - wa[k, pl.ds(r, size), :]
            total = total + (ds[b, pl.ds(r, size), :] - ds[b, pl.ds(r - 1, size), :])
            total = total + back_lane(ds[c, pl.ds(r, size), :])
            dv[k, pl.ds(r, size), :] = dq * da[k, pl.ds(r, size), :] + rb * total
            dw[k, pl.ds(r, size), :] = -rb * here

    def last_stress(c, r, size):
        q = qb[0 if c < 3 else c - 2, pl.ds(r, size), :]
        if c == 0:
            return (cs(2, r, size) + 2.0 * cs(3, r, size)) * q
        return (cs(2, r, size) if c < 3 else cs(3, r, size)) * q

    for r, size in tiles + [(first, 1)]:
        rb, dq = cs(0, r, size), cs(1, r, size)
        full = [last_stress(c, r, size) for c in range(5)]
        totals = [
            full[0] + (full[3] - last_stress(3, r - 1, size)) + back_lane(full[4]),
            full[3] + (full[1] - last_stress(1, r - 1, size)),
            full[4] + back_lane(full[2]),
        ]
        for k in range(3):
            ev[k, pl.ds(r, size), :] = rb * totals[k]
        if r == first:
            continue
        for k in range(3):
            a, b, c = pair_table[k]
            total = es[a, pl.ds(r, size), :] - (msg(2 + right, 3 + k, r, size) + full[a])
            total = total + (es[b, pl.ds(r, size), :] - es[b, pl.ds(r - 1, size), :])
            total = total + back_lane(es[c, pl.ds(r, size), :])
            change = dq * db[k, pl.ds(r, size), :] + rb * total
            vn[k, pl.ds(r, size), :] = has_right * (msg(right, 3 + k, r, size) + change)

    for copy in fetch:
        copy.wait()
    for r, size in tiles:
        out = pl.ds(r - PAD, size)
        at = pl.ds(r, size)
        rl, rm = cs(2, r, size), cs(3, r, size)
        for k in range(3):
            v0[k, 0, out, :] = v0[k, 0, out, :] + dv[k, at, :]
            v0[k, 1, out, :] = v0[k, 1, out, :] + dw[k, at, :]
            v1[k, 0, out, :] = v1[k, 0, out, :] + ev[k, at, :]
        terms = stress_terms(strain_of(dv, r, size, dw), rl, rm)
        for c in range(6):
            s0[c, 0, out, :] = s0[c, 0, out, :] + (ds[c, at, :] + terms[c])
        terms = stress_terms(strain_of(dw, r, size), rl, rm)
        for c in range(6):
            s0[c, 1, out, :] = s0[c, 1, out, :] + terms[c]
        terms = stress_terms(strain_of(ev, r, size, vn), rl, rm)
        for c in range(6):
            more = terms[c] if c == 5 else terms[c] + last_stress(c, r, size)
            s1[c, 1, out, :] = s1[c, 1, out, :] + more
        e = [ev[k, at, :] for k in range(3)]
        spread = rl * e[0]
        for c, more in enumerate((spread + 2.0 * rm * e[0], spread, spread, rm * e[1], rm * e[2])):
            s1[c, 0, out, :] = s1[c, 0, out, :] + more
    for copy in store:
        copy.start()
    for copy in store:
        copy.wait()


def local(velocity, stress, index, table, split, source_x, source_z, source_y, amplitude):
    _, n, m, y = velocity.shape
    f32 = jnp.float32
    high = m + 16
    dma = pltpu.SemaphoreType.DMA
    big = pltpu.CompilerParams(vmem_limit_bytes=40 * 1024 * 1024)
    sources = (source_x, source_z, source_y, amplitude)

    def shape(*dims):
        return jax.ShapeDtypeStruct(dims, f32)

    def cost(flops, moved):
        return pl.CostEstimate(flops=flops, bytes_accessed=moved, transcendentals=0)

    edge_a, edge_b = pl.pallas_call(
        functools.partial(edge_kernel, n, m, y),
        out_shape=[shape(MSG, y)] * 2,
        in_specs=[ANY, ANY, SMEM, SMEM, SMEM],
        out_specs=[VMEM, VMEM],
        scratch_shapes=[pltpu.VMEM((9, n + 1, 8, y), f32)] * 2 + [dma((4,))],
        compiler_params=big,
        name="edge_levels",
    )(velocity, stress, index, table, split)
    got_a, got_b = swap(edge_a, 1, False), swap(edge_b, 1, True)
    levels = pl.pallas_call(
        functools.partial(level_kernel, m),
        out_shape=shape(4, m, y),
        in_specs=[SMEM, SMEM, SMEM],
        out_specs=VMEM,
        compiler_params=big,
        name="level_coefficients",
    )(index, table, split)
    plane_a, plane_b, coef = pl.pallas_call(
        functools.partial(plane_kernel, n, m, y),
        out_shape=[shape(6 * m + 16, y)] * 2 + [shape(4, high, y)],
        in_specs=[ANY, ANY, VMEM, VMEM, VMEM] + [SMEM] * 4,
        out_specs=[ANY, ANY, VMEM],
        scratch_shapes=[
            pltpu.VMEM((MSG, y), f32),
            pltpu.VMEM((MSG, y), f32),
            pltpu.VMEM((6, 3, high, y), f32),
            pltpu.VMEM((3, 2, high, y), f32),
            pltpu.VMEM((6, 2, high, y), f32),
            pltpu.VMEM((3, 2, high, y), f32),
            pltpu.VMEM((2, 6 * m + 16, y), f32),
            dma((4,)),
        ],
        compiler_params=big,
        name="edge_planes",
    )(velocity, stress, got_a, got_b, levels, *sources)
    next_a, next_b = swap(plane_a, 0, False), swap(plane_b, 0, True)
    v_own, s_own = pl.pallas_call(
        functools.partial(main_kernel, n, m, y),
        out_shape=[shape(*velocity.shape), shape(*stress.shape)],
        in_specs=[ANY, ANY, VMEM, VMEM, VMEM] + [SMEM] * 4,
        out_specs=[ANY, ANY],
        scratch_shapes=[
            pltpu.VMEM((MSG, y), f32),
            pltpu.VMEM((MSG, y), f32),
            pltpu.VMEM((6, n + 1, high, y), f32),
            pltpu.VMEM((3, n + 1, high, y), f32),
            pltpu.SMEM((n,), jnp.int32),
            dma((n,)),
            dma((n,)),
            dma((n,)),
            dma((n,)),
        ],
        compiler_params=big,
        cost_estimate=cost(140 * n * m * y, 8 * 9 * n * m * y),
        name="both_steps",
    )(velocity, stress, got_a, got_b, coef, *sources)
    return pl.pallas_call(
        functools.partial(join_kernel, n, m, y),
        out_shape=[shape(*velocity.shape), shape(*stress.shape)],
        in_specs=[ANY] * 4 + [VMEM] + [ANY] * 2,
        out_specs=[ANY, ANY],
        input_output_aliases={5: 0, 6: 1},
        scratch_shapes=[
            pltpu.VMEM((4, 6 * m + 16, y), f32),
            pltpu.VMEM((3, high, y), f32),
            pltpu.VMEM((3, high, y), f32),
            pltpu.VMEM((3, high, y), f32),
            pltpu.VMEM((6, high, y), f32),
            pltpu.VMEM((3, high, y), f32),
            pltpu.VMEM((3, high, y), f32),
            pltpu.VMEM((3, high, y), f32),
            pltpu.VMEM((3, high, y), f32),
            pltpu.VMEM((6, high, y), f32),
            pltpu.VMEM((3, high, y), f32),
            pltpu.VMEM((3, high, y), f32),
            pltpu.VMEM((3, 2, m, y), f32),
            pltpu.VMEM((3, 1, m, y), f32),
            pltpu.VMEM((6, 2, m, y), f32),
            pltpu.VMEM((6, 2, m, y), f32),
            dma((8,)),
        ],
        compiler_params=big,
        name="join_neighbours",
    )(next_a, next_b, plane_a, plane_b, coef, v_own, s_own)


def solution(mesh):
    block = P("member", "horiz", "vert", None)
    return jax.shard_map(
        local,
        mesh=mesh,
        in_specs=(block, block, P("vert"), P(), P(), P(), P(), P(), P("member")),
        out_specs=(block, block),
        check_vma=False,
    )
```

```python
import functools

import jax
import jax.numpy as jnp
from jax import lax
from jax.experimental import pallas as pl
from jax.experimental.pallas import tpu as pltpu
from jax.sharding import PartitionSpec as P

courant = 0.2
wavelet = (1.0, -0.5)
pair_table = ((0, 3, 4), (3, 1, 5), (4, 5, 2))
front = (0, 3, 4)
top = (3, 1, 5)
PAD = 8
ANY = pl.BlockSpec(memory_space=pl.ANY)
HBM = pl.BlockSpec(memory_space=pltpu.HBM)
VMEM = pl.BlockSpec(memory_space=pltpu.VMEM)
SMEM = pl.BlockSpec(memory_space=pltpu.SMEM)


def swap_pairs(rows, cols, along, odd):
    out = []
    for i in range(rows):
        for j in range(cols):
            at, size = (i, rows) if along == 0 else (j, cols)
            if not odd:
                to = at ^ 1
            elif at in (0, size - 1):
                to = None
            else:
                to = at + 1 if at % 2 else at - 1
            if along == 0:
                target = (i, j ^ 1) if to is None else (to, j)
            else:
                target = (i ^ 1, j) if to is None else (i, to)
            out.append((i * cols + j, target[0] * cols + target[1]))
    return out


def swap(block, along, odd):
    rows, cols = lax.axis_size("horiz"), lax.axis_size("vert")
    return lax.ppermute(block, ("horiz", "vert"), swap_pairs(rows, cols, along, odd))


def lane_of(shape):
    return lax.broadcasted_iota(jnp.int32, shape, len(shape) - 1)


def back_lane(a):
    moved = pltpu.roll(a, 1, 1)
    return a - jnp.where(lane_of(a.shape) == 0, 0.0, moved)


def fore_lane(a):
    last = a.shape[-1] - 1
    moved = pltpu.roll(a, last, 1)
    return jnp.where(lane_of(a.shape) == last, 0.0, moved) - a


def velocity_tile(s_at, v_at, rb, dq):
    out = []
    for k in range(3):
        a, b, c = pair_table[k]
        total = (s_at(a, 0, 0) - s_at(a, -1, 0)) + (s_at(b, 0, 0) - s_at(b, 0, -1))
        total = total + back_lane(s_at(c, 0, 0))
        out.append(dq * v_at(k) + rb * total)
    return out


def strain(v_at):
    grads = []
    for i in range(3):
        here = v_at(i, 0, 0)
        grads.append([v_at(i, 1, 0) - here, v_at(i, 0, 1) - here, fore_lane(here)])
    return grads


def stress_terms(g, rl, rm, wanted=range(6)):
    out = {}
    if any(c < 3 for c in wanted):
        spread = rl * (g[0][0] + g[1][1] + g[2][2])
    for c in wanted:
        if c < 3:
            out[c] = spread + 2.0 * rm * g[c][c]
        else:
            i, j = ((0, 1), (0, 2), (1, 2))[c - 3]
            out[c] = rm * (g[i][j] + g[j][i])
    return out


def memo(fn):
    seen = {}

    def call(*key):
        if key not in seen:
            seen[key] = fn(*key)
        return seen[key]

    return call


MSG = 200


def level_scalars(index_ref, table_ref, z):
    kind = index_ref[z]
    return (
        courant * table_ref[0, kind],
        1.0 - courant * table_ref[3, kind],
        courant * table_ref[1, kind],
        courant * table_ref[2, kind],
    )


def edge_kernel(
    n, m, y, v_ref, s_ref, index, table, out_a, out_b, coef, low, high, index_ref, table_ref, sems
):
    vert = lax.axis_index("vert")
    odd = vert % 2 == 1
    copies = []
    for at, (buf, start) in enumerate(((low, 0), (high, m - 8))):
        copies.append(
            pltpu.make_async_copy(s_ref.at[:, :, pl.ds(start, 8), :], buf.at[pl.ds(0, 6), pl.ds(1, n)], sems.at[2 * at])
        )
        copies.append(
            pltpu.make_async_copy(
                v_ref.at[:, :, pl.ds(start, 8), :], buf.at[pl.ds(6, 3), pl.ds(1, n)], sems.at[2 * at + 1]
            )
        )
    scalars = [
        pltpu.make_async_copy(src, dst, sems.at[4 + i])
        for i, (src, dst) in enumerate(((index, index_ref), (table, table_ref)))
    ]
    for copy in scalars + copies:
        copy.start()
    for buf in (low, high):
        for f in front:
            buf[f, 0] = jnp.zeros((8, y), jnp.float32)
    for copy in scalars:
        copy.wait()
    at_first = level_scalars(index_ref, table_ref, 0)
    at_second = level_scalars(index_ref, table_ref, 1)
    at_last = level_scalars(index_ref, table_ref, m - 1)

    def level(z, carry):
        for c, value in enumerate(level_scalars(index_ref, table_ref, z)):
            coef[c, pl.ds(PAD + z, 1), :] = jnp.full((1, y), value, jnp.float32)
        return carry

    lax.fori_loop(0, m, level, 0, unroll=8)
    for copy in copies:
        copy.wait()
    low2 = low.reshape(9 * (n + 1) * 8, y)
    high2 = high.reshape(9 * (n + 1) * 8, y)

    def row(buf, f, z, dx=0):
        return buf[pl.Slice((f * (n + 1) + 1 + dx) * 8 + z, n, 8), :]

    def moved(buf, z, scal):
        return velocity_tile(
            memo(lambda f, dx, dz: row(buf, f, z + dz, dx)), lambda k: row(buf, 6 + k, z), scal[0], scal[1]
        )

    up = [row(high2, f, 7) for f in range(6)] + moved(high2, 7, at_last)
    down = [row(low2, f, 0) for f in range(9)] + moved(low2, 1, at_second)

    def put(at, rows, up_value, down_value):
        out_a[pl.ds(at, rows), :] = jnp.where(odd, down_value, up_value)
        out_b[pl.ds(at, rows), :] = jnp.where(odd, up_value, down_value)

    for f in range(12):
        put(f * n, n, up[f] if f < 9 else down[f], down[f])
    base = 12 * n
    for c in range(4):
        splat = [jnp.full((1, y), a[c], jnp.float32) for a in (at_last, at_first)]
        put(base + c, 1, *splat)
    ahead = jnp.full((1, y), at_second[0], jnp.float32)
    put(base + 4, 1, ahead, ahead)
    for c, f in enumerate(front):
        corner = low[f, n, pl.ds(1, 1), :]
        put(base + 5 + c, 1, corner, corner)


EDGE_MIB, LOAD_MIB, SMALL_MIB = 16, 16, 16
GROUP = 4


def load_kernel(n, m, y, v_ref, s_ref, coef_in, split, vb, sb, coef, sems):
    del coef_in
    body = pl.ds(PAD, m)

    def fetch(g):
        return (
            pltpu.make_async_copy(
                s_ref.at[:, pl.ds(GROUP * g, GROUP)], sb.at[:, pl.ds(GROUP * g + 1, GROUP), body], sems.at[0, g]
            ),
            pltpu.make_async_copy(
                v_ref.at[:, pl.ds(GROUP * g, GROUP)], vb.at[:, pl.ds(GROUP * g + 1, GROUP), body], sems.at[1, g]
            ),
        )

    for g in range(n // GROUP):
        for copy in fetch(g):
            copy.start()
    for f in front:
        sb[f, 0] = jnp.zeros((m + 16, y), jnp.float32)
    for k in range(3):
        vb[k, n + 1] = jnp.zeros((m + 16, y), jnp.float32)
    high = m + 16
    s2 = sb.reshape(6 * (n + 1) * high, y)
    for f in top:
        s2[pl.Slice((f * (n + 1) + 1) * high + PAD - 1, n, high), :] = jnp.zeros((n, y), jnp.float32)

    lowest, first = PAD - 1, PAD + m
    coef[3, pl.ds(lowest, 1), :] = jnp.ones((1, y), jnp.float32)
    coef[3, pl.ds(first, 1), :] = jnp.ones((1, y), jnp.float32)
    start = split[0] - lax.axis_index("vert") * m
    for r, size in [(PAD + 8 * t, 8) for t in range(m // 8)] + [(lowest, 1), (first, 1)]:
        level = r - PAD + lax.broadcasted_iota(jnp.int32, (size, y), 0)
        at = pl.ds(r, size)
        coef[3, at, :] = jnp.where(level >= start, coef[3, at, :], 0.0)

    def advance(g, carry):
        for copy in fetch(g):
            copy.wait()
        for p in range(GROUP):
            x = GROUP * g + p
            for t in range(m // 8):
                r = PAD + 8 * t
                new = velocity_tile(
                    memo(lambda f, dx, dz: sb[f, x + 1 + dx, pl.ds(r + dz, 8), :]),
                    lambda k: vb[k, x + 1, pl.ds(r, 8), :],
                    coef[0, pl.ds(r, 8), :],
                    coef[1, pl.ds(r, 8), :],
                )
                for k in range(3):
                    vb[k, x + 1, pl.ds(r, 8), :] = new[k]
        return carry

    lax.fori_loop(0, n // GROUP, advance, 0)


def fetch_sources(refs, held, sems):
    copies = [pltpu.make_async_copy(src, dst, sems.at[i]) for i, (src, dst) in enumerate(zip(refs, held))]
    for copy in copies:
        copy.start()
    return copies


def add_sources(add_row, plane_of, z_low, z_high, scale, x_at, z_at, src):
    sx, sz, sy, amp = src

    def body(i, carry):
        x, z = sx[i] - x_at, sz[i] - z_at

        @pl.when(plane_of(x) & (z >= z_low) & (z < z_high))
        def _():
            lane = lane_of((1, 128))
            add_row(x, z, jnp.where(lane == sy[i], scale * amp[i], 0.0))

        return carry

    lax.fori_loop(0, sx.shape[0], body, 0)


def plane_kernel(
    n, m, y, got_a, got_b, vb, sb, coef_in, *refs
):
    sources, (out_a, out_b, below, above, coef), scratch = refs[:4], refs[4:9], refs[9:]
    sl, vl, sr, vr, msg, sx, sz, sy, amp, sems = scratch
    del coef_in
    horiz, vert = lax.axis_index("horiz"), lax.axis_index("vert")
    fetched = fetch_sources(sources, (sx, sz, sy, amp), sems)
    odd = vert % 2 == 1
    has_below = jnp.where(vert > 0, 1.0, 0.0)
    has_above = jnp.where(vert < lax.axis_size("vert") - 1, 1.0, 0.0)
    for t in range(MSG // 8):
        at = pl.ds(8 * t, 8)
        a, b = got_a[at, :], got_b[at, :]
        below[at, :] = has_below * jnp.where(odd, a, b)
        above[at, :] = has_above * jnp.where(odd, b, a)
    lowest, first, second = PAD - 1, PAD + m, PAD + m + 1
    base = 12 * n
    for c in range(4):
        for r, side in ((lowest, below), (first, above)):
            value = side[pl.ds(base + c, 1), :]
            coef[c, pl.ds(r, 1), :] = value * coef[c, pl.ds(r, 1), :] if c == 3 else value
    coef[0, pl.ds(second, 1), :] = above[pl.ds(base + 4, 1), :]

    tiles = [(PAD + 8 * t, 8) for t in range(m // 8)]
    right, left = horiz % 2, 1 - horiz % 2
    tail = 6 * m

    def cs(c, r, size):
        return coef[c, pl.ds(r, size), :]

    def from_below(f, x):
        return below[pl.ds(f * n + x, 1), :]

    def from_above(f, x):
        return above[pl.ds(f * n + x, 1), :]

    for x, buf, at in ((0, vl, 0), (1, vl, 1), (n - 1, vr, 0)):
        for k in range(3):
            for r, size in tiles:
                buf[k, at, pl.ds(r, size), :] = vb[k, x + 1, pl.ds(r, size), :]
            line = pl.ds(PAD, 1)
            buf[k, at, line, :] = vb[k, x + 1, line, :] - cs(0, PAD, 1) * from_below(top[k], x)
            buf[k, at, pl.ds(lowest, 1), :] = from_below(6 + k, x)
            buf[k, at, pl.ds(second, 1), :] = from_above(9 + k, x)

        def beyond(f, dx, dz):
            if dz:
                return sb[f, x + 1, pl.ds(first - 1, 1), :]
            if x + dx < 0:
                return jnp.zeros((1, y), jnp.float32)
            return from_above(f, x + dx)

        new = velocity_tile(memo(beyond), lambda k: from_above(6 + k, x), cs(0, first, 1), cs(1, first, 1))
        for k in range(3):
            buf[k, at, pl.ds(first, 1), :] = new[k]

    def stress_rows(f, x, r, size):
        if r < PAD:
            return from_below(f, x)
        if r >= first:
            return from_above(f, x)
        return sb[f, x + 1, pl.ds(r, size), :]

    def load(out, v_buf, x, r, size, wanted, ahead):
        def at(k, dx, dz):
            if dx and not ahead:
                return 0.0
            return v_buf[k, dx, pl.ds(r + dz, size), :]

        terms = stress_terms(strain(memo(at)), cs(2, r, size), cs(3, r, size), wanted)
        for c in wanted:
            out[c, pl.ds(r, size), :] = stress_rows(c, x, r, size) + terms[c]

    for r, size in tiles + [(first, 1)]:
        load(sr, vr, n - 1, r, size, front, False)
    load(sl, vl, 0, lowest, 1, top, True)
    for r, size in tiles:
        load(sl, vl, 0, r, size, range(6), True)
    for c, f in enumerate(front):
        for r, size in tiles:
            msg[right, pl.ds(c * m + r - PAD, size), :] = sb[f, n, pl.ds(r, size), :]
            msg[left, pl.ds(c * m + r - PAD, size), :] = vl[c, 0, pl.ds(r, size), :]
        msg[right, pl.ds(tail + c, 1), :] = from_below(f, n - 1)
        msg[right, pl.ds(tail + 3 + c, 1), :] = from_above(f, n - 1)
        msg[right, pl.ds(tail + 6 + c, 1), :] = above[pl.ds(base + 5 + c, 1), :]
        msg[left, pl.ds(tail + c, 1), :] = vl[c, 0, pl.ds(lowest, 1), :]
        msg[left, pl.ds(tail + 3 + c, 1), :] = vl[c, 0, pl.ds(first, 1), :]

    for copy in fetched:
        copy.wait()

    def add(x, z, row):
        at = pl.ds(PAD + z, 1)

        @pl.when(x == 0)
        def _():
            for c in range(3):
                sl[c, at, :] = sl[c, at, :] + row

        @pl.when(x == n - 1)
        def _():
            sr[0, at, :] = sr[0, at, :] + row

    add_sources(
        add, lambda x: (x == 0) | (x == n - 1), -1, m + 1, courant * wavelet[0], horiz * n, vert * m, (sx, sz, sy, amp)
    )
    for c, f in enumerate(front):
        for r, size in tiles:
            msg[right, pl.ds((3 + c) * m + r - PAD, size), :] = sr[f, pl.ds(r, size), :]
        msg[right, pl.ds(tail + 9 + c, 1), :] = sr[f, pl.ds(first, 1), :]
    for r, size in tiles:
        new = velocity_tile(
            memo(lambda f, dx, dz: 0.0 if dx else sl[f, pl.ds(r + dz, size), :]),
            lambda k: vl[k, 0, pl.ds(r, size), :],
            cs(0, r, size),
            cs(1, r, size),
        )
        for k in range(3):
            msg[left, pl.ds((3 + k) * m + r - PAD, size), :] = new[k]
    for t in range((6 * m + 16) // 8):
        at = pl.ds(8 * t, 8)
        out_a[at, :] = msg[0, at, :]
        out_b[at, :] = msg[1, at, :]


def rest_kernel(n, m, y, v_in, s_in, below, above, coef, *refs):
    sources, (vb, sb, out_v, out_s), scratch = refs[:4], refs[4:8], refs[8:]
    sx, sz, sy, amp, near_x, near_z, near_y, near_amp, small, sems = scratch
    del v_in, s_in
    horiz, vert = lax.axis_index("horiz"), lax.axis_index("vert")
    fetched = fetch_sources(sources, (sx, sz, sy, amp), small)
    body = pl.ds(PAD, m)
    lowest, first, second = PAD - 1, PAD + m, PAD + m + 1
    high = m + 16
    s2 = sb.reshape(6 * (n + 1) * high, y)
    v2 = vb.reshape(3 * (n + 2) * high, y)
    tiles = [(PAD + 8 * t, 8) for t in range(m // 8)]

    def cs(c, r, size):
        return coef[c, pl.ds(r, size), :]

    def s_line(f, r):
        return pl.Slice((f * (n + 1) + 1) * high + r, n, high)

    def v_line(k, r):
        return pl.Slice((k * (n + 2) + 1) * high + r, n, high)

    def beyond(f, dx, dz):
        if dz:
            return s2[s_line(f, first - 1), :]
        here = above[pl.ds(f * n, n), :]
        if dx:
            rows = lax.broadcasted_iota(jnp.int32, (n, y), 0)
            return jnp.where(rows == 0, 0.0, pltpu.roll(here, 1, 0))
        return here

    new = velocity_tile(
        memo(beyond), lambda k: above[pl.ds((6 + k) * n, n), :], cs(0, first, 1), cs(1, first, 1)
    )
    for k in range(3):
        v2[v_line(k, first), :] = new[k]
        v2[v_line(k, lowest), :] = below[pl.ds((6 + k) * n, n), :]
        v2[v_line(k, second), :] = above[pl.ds((9 + k) * n, n), :]
        v2[v_line(k, PAD), :] = v2[v_line(k, PAD), :] - cs(0, PAD, 1) * below[pl.ds(top[k] * n, n), :]
    for f in range(6):
        s2[s_line(f, lowest), :] = below[pl.ds(f * n, n), :]
        s2[s_line(f, first), :] = above[pl.ds(f * n, n), :]

    def move(x):
        for r, size in tiles + [(first, 1)]:
            new = velocity_tile(
                memo(lambda f, dx, dz: sb[f, x + 1 + dx, pl.ds(r + dz, size), :]),
                lambda k: vb[k, x + 1, pl.ds(r, size), :],
                cs(0, r, size),
                cs(1, r, size),
            )
            for k in range(3):
                vb[k, x + 1, pl.ds(r, size), :] = new[k]

    def load(x, step):
        parts = [(r, size, range(6)) for r, size in tiles]
        if step == 0:
            parts += [(lowest, 1, top), (first, 1, range(6))]
        for r, size, wanted in parts:
            g = strain(memo(lambda k, dx, dz: vb[k, x + 1 + dx, pl.ds(r + dz, size), :]))
            terms = stress_terms(g, cs(2, r, size), cs(3, r, size), wanted)
            for c in wanted:
                sb[c, x + 1, pl.ds(r, size), :] = sb[c, x + 1, pl.ds(r, size), :] + terms[c]

    for copy in fetched:
        copy.wait()
    found = jnp.int32(0)
    for i in range(sx.shape[0]):
        x, z = sx[i] - horiz * n, sz[i] - vert * m
        near_x[found], near_z[found], near_y[found], near_amp[found] = x, z, sy[i], amp[i]
        found = found + ((x >= 0) & (x < n) & (z >= -1) & (z <= m)).astype(jnp.int32)

    def add_near(step, x_low, x_high, z_low, z_high):
        def add(j, carry):
            x, z = near_x[j], near_z[j]

            @pl.when((x >= x_low) & (x < x_high) & (z >= z_low) & (z < z_high))
            def _():
                row = jnp.where(lane_of((1, y)) == near_y[j], courant * wavelet[step] * near_amp[j], 0.0)
                at = pl.ds(PAD + z, 1)
                for c in range(3):
                    sb[c, x + 1, at, :] = sb[c, x + 1, at, :] + row

            return carry

        lax.fori_loop(0, found, add, 0)

    def v_off(x):
        return pltpu.make_async_copy(vb.at[:, x + 1, body], out_v.at[:, x], sems.at[0, x])

    def s_off(x):
        return pltpu.make_async_copy(sb.at[:, x + 1, body], out_s.at[:, x], sems.at[1, x])

    def send(off, x, end):
        @pl.when((x >= 2) & (x < end))
        def _():
            off(x).start()

    add_near(0, 0, n, -1, m + 1)

    def advance(g, carry):
        x = GROUP * g
        for p in range(GROUP):
            load(x + p, 0)
        for p in range(GROUP):
            move(x + p)
        for p in range(GROUP):
            send(v_off, x + p, n - 2)
        for p in range(-1, GROUP - 1):
            load(x + p, 1)
        add_near(1, x - 1, x + GROUP - 1, 0, m)
        for p in range(-1, GROUP - 1):
            send(s_off, x + p, n - 1 - GROUP)
        return carry

    lax.fori_loop(0, n // GROUP, advance, 0)
    load(n - 1, 1)
    add_near(1, n - 1, n, 0, m)

    def finish(x, carry):
        v_off(x).wait()

        @pl.when(x < n - 1 - GROUP)
        def _():
            s_off(x).wait()

        return carry

    lax.fori_loop(2, n - 2, finish, 0)


def join_kernel(n, m, y, next_a, next_b, own_a, own_b, coef, vb, sb, v_in, s_in, v_out, s_out, *scratch):
    wa, da, ds, dv, dw, qb, db, es, ev, vn, v0, v1, s0, s1, sems = scratch
    del v_in, s_in
    horiz = lax.axis_index("horiz")
    even = horiz % 2 == 0
    has_left = jnp.where(horiz > 0, 1.0, 0.0)
    has_right = jnp.where(horiz < lax.axis_size("horiz") - 1, 1.0, 0.0)
    lowest, first, second = PAD - 1, PAD + m, PAD + m + 1
    tail = 6 * m
    tiles = [(PAD + 8 * t, 8) for t in range(m // 8)]

    def cs(c, r, size):
        return coef[c, pl.ds(r, size), :]

    pick = {"right": (next_a, next_b), "left": (next_b, next_a), "own right": (own_a, own_b), "own left": (own_b, own_a)}

    def rows_of(which, at, size):
        a, b = pick[which]
        return jnp.where(even, a[pl.ds(at, size), :], b[pl.ds(at, size), :])

    def msg(which, c, r, size):
        return rows_of(which, c * m + r - PAD, size)

    def end(which, at):
        return rows_of(which, tail + at, 1)

    for k in range(3):
        rows = [(r, size, msg("left", k, r, size)) for r, size in tiles]
        rows += [(r, 1, end("left", at + k)) for r, at in ((lowest, 0), (first, 3), (second, 6))]
        for r, size, value in rows:
            da[k, pl.ds(r, size), :] = -(has_left * cs(0, r, size)) * value
        rows = [(r, size, msg("left", 3 + k, r, size), msg("own left", k, r, size)) for r, size in tiles]
        rows += [(first, 1, end("left", 9 + k), end("own left", 3 + k))]
        for r, size, value, own in rows:
            gain = cs(3, r, size) if k else cs(2, r, size) + 2.0 * cs(3, r, size)
            wa[k, pl.ds(r, size), :] = has_left * (value + gain * (own + da[k, pl.ds(r, size), :]))
        rows = [(r, size, msg("own right", k, r, size), msg("right", k, r, size)) for r, size in tiles]
        rows += [(r, 1, end("own right", at + k), end("right", at + k)) for r, at in ((lowest, 0), (first, 3))]
        for r, size, value, other in rows:
            change = -(has_right * cs(0, r, size)) * value
            db[k, pl.ds(r, size), :] = change
            qb[k, pl.ds(r, size), :] = has_right * other + change

    def strain_of(buf, r, size, ahead=None):
        grads = []
        for i in range(3):
            here = buf[i, pl.ds(r, size), :]
            beyond = -here if ahead is None else ahead[i, pl.ds(r, size), :] - here
            grads.append([beyond, buf[i, pl.ds(r + 1, size), :] - here, fore_lane(here)])
        return grads

    for out, src, ends in ((ds, da, (lowest, first)), (es, db, (lowest,))):
        parts = [(r, size, range(6)) for r, size in tiles]
        parts += [(r, 1, top if r == lowest else range(6)) for r in ends]
        for r, size, wanted in parts:
            terms = stress_terms(strain_of(src, r, size), cs(2, r, size), cs(3, r, size), wanted)
            for c in wanted:
                out[c, pl.ds(r, size), :] = terms[c]

    for r, size in tiles + [(first, 1)]:
        rb, dq = cs(0, r, size), cs(1, r, size)
        for k in range(3):
            a, b, c = pair_table[k]
            here = ds[a, pl.ds(r, size), :]
            total = here - wa[k, pl.ds(r, size), :]
            total = total + (ds[b, pl.ds(r, size), :] - ds[b, pl.ds(r - 1, size), :])
            total = total + back_lane(ds[c, pl.ds(r, size), :])
            dv[k, pl.ds(r, size), :] = dq * da[k, pl.ds(r, size), :] + rb * total
            dw[k, pl.ds(r, size), :] = -rb * here

    def last_stress(c, r, size):
        q = qb[0 if c < 3 else c - 2, pl.ds(r, size), :]
        if c == 0:
            return (cs(2, r, size) + 2.0 * cs(3, r, size)) * q
        return (cs(2, r, size) if c < 3 else cs(3, r, size)) * q

    for r, size in tiles + [(first, 1)]:
        rb, dq = cs(0, r, size), cs(1, r, size)
        full = [last_stress(c, r, size) for c in range(5)]
        totals = [
            full[0] + (full[3] - last_stress(3, r - 1, size)) + back_lane(full[4]),
            full[3] + (full[1] - last_stress(1, r - 1, size)),
            full[4] + back_lane(full[2]),
        ]
        for k in range(3):
            ev[k, pl.ds(r, size), :] = rb * totals[k]
        if r == first:
            continue
        for k in range(3):
            a, b, c = pair_table[k]
            total = es[a, pl.ds(r, size), :] - (msg("own right", 3 + k, r, size) + full[a])
            total = total + (es[b, pl.ds(r, size), :] - es[b, pl.ds(r - 1, size), :])
            total = total + back_lane(es[c, pl.ds(r, size), :])
            change = dq * db[k, pl.ds(r, size), :] + rb * total
            vn[k, pl.ds(r, size), :] = has_right * (msg("right", 3 + k, r, size) + change)

    def put(buf, dst, x, i):
        copy = pltpu.make_async_copy(buf, dst.at[:, x], sems.at[i])
        copy.start()
        return copy

    rest = pltpu.make_async_copy(
        sb.at[:, pl.ds(n - GROUP, GROUP - 1), pl.ds(PAD, m)], s_out.at[:, pl.ds(n - 1 - GROUP, GROUP - 1)], sems.at[8]
    )
    rest.start()
    copies = [rest]
    for buf, x, change in ((v0.at[:, 0], 0, dv), (v0.at[:, 1], 1, dw), (v1.at[:, 0], n - 1, ev), (v1.at[:, 1], n - 2, None)):
        for r, size in tiles:
            out, at = pl.ds(r - PAD, size), pl.ds(r, size)
            for k in range(3):
                old = vb[k, x + 1, at, :]
                buf[k, out, :] = old if change is None else old + change[k, at, :]
        copies.append(put(buf, v_out, x, len(copies) - 1))
    for buf, x, src, ahead, more in (
        (s0.at[:, 0], 0, dv, dw, lambda c, r: ds[c, pl.ds(r, 8), :]),
        (s0.at[:, 1], 1, dw, None, None),
        (s1.at[:, 0], n - 1, ev, vn, lambda c, r: None if c == 5 else last_stress(c, r, 8)),
    ):
        for r, size in tiles:
            out, at = pl.ds(r - PAD, size), pl.ds(r, size)
            terms = stress_terms(strain_of(src, r, size, ahead), cs(2, r, size), cs(3, r, size))
            for c in range(6):
                extra = None if more is None else more(c, r)
                term = terms[c] if extra is None else terms[c] + extra
                buf[c, out, :] = sb[c, x + 1, at, :] + term
        copies.append(put(buf, s_out, x, len(copies) - 1))
    for r, size in tiles:
        out, at = pl.ds(r - PAD, size), pl.ds(r, size)
        rl, rm = cs(2, r, size), cs(3, r, size)
        e = [ev[k, at, :] for k in range(3)]
        spread = rl * e[0]
        for c, term in enumerate((spread + 2.0 * rm * e[0], spread, spread, rm * e[1], rm * e[2], None)):
            old = sb[c, n - 1, at, :]
            s1[c, 1, out, :] = old if term is None else old + term
    copies.append(put(s1.at[:, 1], s_out, n - 2, len(copies) - 1))
    for copy in copies:
        copy.wait()


def local(velocity, stress, index, table, split, source_x, source_z, source_y, amplitude):
    _, n, m, y = velocity.shape
    f32, i32 = jnp.float32, jnp.int32
    high = m + 16
    dma = pltpu.SemaphoreType.DMA
    sources = (source_x, source_z, source_y, amplitude)
    held = [pltpu.SMEM(a.shape, a.dtype) for a in sources]
    near = [pltpu.SMEM((a.shape[0] + 1,), a.dtype) for a in sources]
    table = table.T
    materials = [pltpu.SMEM((m,), i32), pltpu.SMEM(table.shape, f32)]

    def shape(*dims):
        return jax.ShapeDtypeStruct(dims, f32)

    def kept(*dims):
        return pltpu.VMEM(dims, f32)

    def outside(*dims):
        return pltpu.HBM(dims, f32)

    def room(mib):
        return pltpu.CompilerParams(vmem_limit_bytes=mib * 1024 * 1024)

    def cost(flops, moved):
        return pl.CostEstimate(flops=flops, bytes_accessed=moved, transcendentals=0)

    padded_v, padded_s = kept(3, n + 2, high, y), kept(6, n + 1, high, y)
    edge_a, edge_b, coef = pl.pallas_call(
        functools.partial(edge_kernel, n, m, y),
        out_shape=[kept(MSG, y)] * 2 + [kept(4, high, y)],
        in_specs=[HBM] * 4,
        out_specs=[VMEM] * 3,
        scratch_shapes=[pltpu.VMEM((9, n + 1, 8, y), f32)] * 2 + materials + [dma((6,))],
        compiler_params=room(EDGE_MIB),
        name="edge_levels",
    )(*[pltpu.with_memory_space_constraint(a, pltpu.HBM) for a in (velocity, stress, index, table)])
    got_a, got_b = swap(edge_a, 1, False), swap(edge_b, 1, True)
    split, edge_a = lax.optimization_barrier((split, edge_a))
    vb, sb, coef = pl.pallas_call(
        functools.partial(load_kernel, n, m, y),
        out_shape=[padded_v, padded_s, kept(4, high, y)],
        in_specs=[ANY, ANY, VMEM, SMEM],
        out_specs=[VMEM] * 3,
        input_output_aliases={2: 2},
        scratch_shapes=[dma((2, n // GROUP))],
        compiler_params=room(LOAD_MIB),
        cost_estimate=cost(30 * n * m * y, 4 * 9 * n * m * y),
        name="load_block",
    )(velocity, stress, coef, split)
    plane_a, plane_b, below, above, coef = pl.pallas_call(
        functools.partial(plane_kernel, n, m, y),
        out_shape=[kept(6 * m + 16, y)] * 2 + [kept(MSG, y)] * 2 + [kept(4, high, y)],
        in_specs=[VMEM] * 5 + [ANY] * 4,
        out_specs=[VMEM] * 5,
        input_output_aliases={4: 4},
        scratch_shapes=[
            pltpu.VMEM((6, high, y), f32),
            pltpu.VMEM((3, 2, high, y), f32),
            pltpu.VMEM((6, high, y), f32),
            pltpu.VMEM((3, 1, high, y), f32),
            pltpu.VMEM((2, 6 * m + 16, y), f32),
            *held,
            dma((4,)),
        ],
        compiler_params=room(SMALL_MIB),
        name="edge_planes",
    )(got_a, got_b, vb, sb, coef, *sources)
    next_a, next_b = swap(plane_a, 0, False), swap(plane_b, 0, True)
    vb, sb, v_own, s_own = pl.pallas_call(
        functools.partial(rest_kernel, n, m, y),
        out_shape=[padded_v, padded_s, outside(*velocity.shape), outside(*stress.shape)],
        in_specs=[VMEM] * 5 + [ANY] * 4,
        out_specs=[VMEM, VMEM, HBM, HBM],
        input_output_aliases={0: 0, 1: 1},
        scratch_shapes=[*held, *near, dma((4,)), dma((2, n))],
        compiler_params=room(SMALL_MIB),
        cost_estimate=cost(110 * n * m * y, 4 * 9 * n * m * y),
        name="both_steps",
    )(vb, sb, below, above, coef, *sources)
    plane = pltpu.VMEM((3, high, y), f32)
    plane6 = pltpu.VMEM((6, high, y), f32)
    return pl.pallas_call(
        functools.partial(join_kernel, n, m, y),
        out_shape=[outside(*velocity.shape), outside(*stress.shape)],
        in_specs=[VMEM] * 7 + [HBM] * 2,
        out_specs=[HBM, HBM],
        input_output_aliases={7: 0, 8: 1},
        scratch_shapes=[plane, plane, plane6, plane, plane, plane, plane, plane6, plane, plane]
        + [pltpu.VMEM((3, 2, m, y), f32)] * 2
        + [pltpu.VMEM((6, 2, m, y), f32)] * 2
        + [dma((9,))],
        compiler_params=room(SMALL_MIB),
        name="join_neighbours",
    )(next_a, next_b, plane_a, plane_b, coef, vb, sb, v_own, s_own)


def solution(mesh):
    block = P("member", "horiz", "vert", None)
    return jax.shard_map(
        local,
        mesh=mesh,
        in_specs=(block, block, P("vert"), P(), P(), P(), P(), P(), P("member")),
        out_specs=(block, block),
        check_vma=False,
    )
```

```python
import functools

import jax
import jax.numpy as jnp
from jax import lax
from jax.experimental import pallas as pl
from jax.experimental.pallas import tpu as pltpu
from jax.sharding import PartitionSpec as P

courant = 0.2
wavelet = (1.0, -0.5)
pair_table = ((0, 3, 4), (3, 1, 5), (4, 5, 2))
front = (0, 3, 4)
top = (3, 1, 5)
PAD = 8
ANY = pl.BlockSpec(memory_space=pl.ANY)
HBM = pl.BlockSpec(memory_space=pltpu.HBM)
VMEM = pl.BlockSpec(memory_space=pltpu.VMEM)
SMEM = pl.BlockSpec(memory_space=pltpu.SMEM)


def swap_pairs(sizes, along, odd):
    members, rows, cols = sizes
    out = []
    for a in range(members):
        for i in range(rows):
            for j in range(cols):
                here = [a, i, j]
                there = [a, i, j]
                if not odd:
                    there[along] ^= 1
                elif 0 < here[along] < sizes[along] - 1:
                    there[along] += 1 if here[along] % 2 else -1
                else:
                    there[1 if along == 2 else 2 if members % 2 else 0] ^= 1
                out.append(tuple((p[0] * rows + p[1]) * cols + p[2] for p in (here, there)))
    return out


def swap(block, along, odd):
    axes = ("member", "horiz", "vert")
    return lax.ppermute(block, axes, swap_pairs([lax.axis_size(a) for a in axes], along, odd))


def lane_of(shape):
    return lax.broadcasted_iota(jnp.int32, shape, len(shape) - 1)


def back_lane(a):
    moved = pltpu.roll(a, 1, 1)
    return a - jnp.where(lane_of(a.shape) == 0, 0.0, moved)


def fore_lane(a):
    last = a.shape[-1] - 1
    moved = pltpu.roll(a, last, 1)
    return jnp.where(lane_of(a.shape) == last, 0.0, moved) - a


def velocity_tile(s_at, v_at, rb, dq):
    out = []
    for k in range(3):
        a, b, c = pair_table[k]
        total = (s_at(a, 0, 0) - s_at(a, -1, 0)) + (s_at(b, 0, 0) - s_at(b, 0, -1))
        total = total + back_lane(s_at(c, 0, 0))
        out.append(dq * v_at(k) + rb * total)
    return out


def strain(v_at):
    grads = []
    for i in range(3):
        here = v_at(i, 0, 0)
        grads.append([v_at(i, 1, 0) - here, v_at(i, 0, 1) - here, fore_lane(here)])
    return grads


def stress_terms(g, rl, rm, wanted=range(6)):
    out = {}
    if any(c < 3 for c in wanted):
        spread = rl * (g[0][0] + g[1][1] + g[2][2])
    for c in wanted:
        if c < 3:
            out[c] = spread + 2.0 * rm * g[c][c]
        else:
            i, j = ((0, 1), (0, 2), (1, 2))[c - 3]
            out[c] = rm * (g[i][j] + g[j][i])
    return out


def memo(fn):
    seen = {}

    def call(*key):
        if key not in seen:
            seen[key] = fn(*key)
        return seen[key]

    return call


MSG = 200


def level_scalars(index_ref, table_ref, z):
    kind = index_ref[z]
    return (
        courant * table_ref[0, kind],
        1.0 - courant * table_ref[3, kind],
        courant * table_ref[1, kind],
        courant * table_ref[2, kind],
    )


def edge_kernel(
    n, m, y, v_ref, s_ref, index, table, out_a, out_b, coef, low, high, index_ref, table_ref, sems
):
    vert = lax.axis_index("vert")
    odd = vert % 2 == 1
    copies = []
    for at, (buf, start) in enumerate(((low, 0), (high, m - 8))):
        copies.append(
            pltpu.make_async_copy(s_ref.at[:, :, pl.ds(start, 8), :], buf.at[pl.ds(0, 6), pl.ds(1, n)], sems.at[2 * at])
        )
        copies.append(
            pltpu.make_async_copy(
                v_ref.at[:, :, pl.ds(start, 8), :], buf.at[pl.ds(6, 3), pl.ds(1, n)], sems.at[2 * at + 1]
            )
        )
    scalars = [
        pltpu.make_async_copy(src, dst, sems.at[4 + i])
        for i, (src, dst) in enumerate(((index, index_ref), (table, table_ref)))
    ]
    for copy in scalars + copies:
        copy.start()
    for buf in (low, high):
        for f in front:
            buf[f, 0] = jnp.zeros((8, y), jnp.float32)
    for copy in scalars:
        copy.wait()
    at_first = level_scalars(index_ref, table_ref, 0)
    at_second = level_scalars(index_ref, table_ref, 1)
    at_last = level_scalars(index_ref, table_ref, m - 1)

    def level(z, carry):
        for c, value in enumerate(level_scalars(index_ref, table_ref, z)):
            coef[c, pl.ds(PAD + z, 1), :] = jnp.full((1, y), value, jnp.float32)
        return carry

    lax.fori_loop(0, m, level, 0, unroll=8)
    for copy in copies:
        copy.wait()
    low2 = low.reshape(9 * (n + 1) * 8, y)
    high2 = high.reshape(9 * (n + 1) * 8, y)

    def row(buf, f, z, dx=0):
        return buf[pl.Slice((f * (n + 1) + 1 + dx) * 8 + z, n, 8), :]

    def moved(buf, z, scal):
        return velocity_tile(
            memo(lambda f, dx, dz: row(buf, f, z + dz, dx)), lambda k: row(buf, 6 + k, z), scal[0], scal[1]
        )

    up = [row(high2, f, 7) for f in range(6)] + moved(high2, 7, at_last)
    down = [row(low2, f, 0) for f in range(9)] + moved(low2, 1, at_second)

    def put(at, rows, up_value, down_value):
        out_a[pl.ds(at, rows), :] = jnp.where(odd, down_value, up_value)
        out_b[pl.ds(at, rows), :] = jnp.where(odd, up_value, down_value)

    for f in range(12):
        put(f * n, n, up[f] if f < 9 else down[f], down[f])
    base = 12 * n
    for c in range(4):
        splat = [jnp.full((1, y), a[c], jnp.float32) for a in (at_last, at_first)]
        put(base + c, 1, *splat)
    ahead = jnp.full((1, y), at_second[0], jnp.float32)
    put(base + 4, 1, ahead, ahead)
    for c, f in enumerate(front):
        corner = low[f, n, pl.ds(1, 1), :]
        put(base + 5 + c, 1, corner, corner)


EDGE_MIB, LOAD_MIB, SMALL_MIB = 16, 16, 16
GROUP = 4


def load_kernel(n, m, y, v_ref, s_ref, coef_in, split, *refs):
    sources, (vb, sb, raw, coef), scratch = refs[:4], refs[4:8], refs[8:]
    sx, sz, sy, amp, small = scratch
    del coef_in
    fetched = fetch_sources(sources, (sx, sz, sy, amp), small)
    for f in front:
        sb[f, 0] = jnp.zeros((m + 16, y), jnp.float32)
    for k in range(3):
        vb[k, n + 1] = jnp.zeros((m + 16, y), jnp.float32)
    lowest, first = PAD - 1, PAD + m
    s_line, v_line, s2, v2 = lines(n, m, y, vb, sb)
    zero = jnp.zeros((n, y), jnp.float32)
    for f in range(6):
        s2[s_line(f, lowest), :] = zero
        s2[s_line(f, first), :] = zero
    for k in range(3):
        v2[v_line(k, first), :] = zero
    coef[3, pl.ds(lowest, 1), :] = jnp.ones((1, y), jnp.float32)
    coef[3, pl.ds(first, 1), :] = jnp.ones((1, y), jnp.float32)
    start = split[0] - lax.axis_index("vert") * m
    tiles = [PAD + 8 * t for t in range(m // 8)]
    for r, size in [(r, 8) for r in tiles] + [(lowest, 1), (first, 1)]:
        level = r - PAD + lax.broadcasted_iota(jnp.int32, (size, y), 0)
        at = pl.ds(r, size)
        coef[3, at, :] = jnp.where(level >= start, coef[3, at, :], 0.0)

    def cs(c, r):
        return coef[c, pl.ds(r, 8), :]

    def move(x, has_before):
        for r in tiles:

            def stress_at(f, dx, dz):
                if dx and not has_before:
                    return 0.0
                if dz and r == PAD:
                    return plane_before(s_ref[f, x, pl.ds(0, 8), :])
                return s_ref[f, x + dx, pl.ds(r - PAD + dz, 8), :]

            new = velocity_tile(memo(stress_at), lambda k: v_ref[k, x, pl.ds(r - PAD, 8), :], cs(0, r), cs(1, r))
            for k in range(3):
                vb[k, x + 1, pl.ds(r, 8), :] = new[k]

    def load(x):
        for r in tiles:
            grads = strain(memo(lambda k, dx, dz: vb[k, x + 1 + dx, pl.ds(r + dz, 8), :]))
            terms = stress_terms(grads, cs(2, r), cs(3, r))
            for c in range(6):
                sb[c, x + 1, pl.ds(r, 8), :] = s_ref[c, x, pl.ds(r - PAD, 8), :] + terms[c]

    def sweep(work, start):
        def go(g, carry):
            for p in range(GROUP):
                work(GROUP * g + p)
            return carry

        lax.fori_loop(start, n // GROUP, go, 0)

    for x in range(GROUP):
        move(x, x > 0)
    sweep(lambda x: move(x, True), 1)
    sweep(load, 0)
    for c, f in enumerate(front):
        raw[c] = s_ref[f, n - 1]
    for copy in fetched:
        copy.wait()
    x_at, z_at = lax.axis_index("horiz") * n, lax.axis_index("vert") * m

    def add(i, carry):
        x, z = sx[i] - x_at, sz[i] - z_at

        @pl.when((x >= 0) & (x < n) & (z >= -1) & (z <= m))
        def _():
            row = jnp.where(lane_of((1, y)) == sy[i], courant * wavelet[0] * amp[i], 0.0)
            at = pl.ds(PAD + z, 1)
            for c in range(3):
                sb[c, x + 1, at, :] = sb[c, x + 1, at, :] + row

        return carry

    lax.fori_loop(0, sx.shape[0], add, 0)


def lines(n, m, y, vb, sb):
    high = m + 16

    def s_line(f, r):
        return pl.Slice((f * (n + 1) + 1) * high + r, n, high)

    def v_line(k, r):
        return pl.Slice((k * (n + 2) + 1) * high + r, n, high)

    return s_line, v_line, sb.reshape(6 * (n + 1) * high, y), vb.reshape(3 * (n + 2) * high, y)


def plane_before(a):
    rows = lax.broadcasted_iota(jnp.int32, a.shape, 0)
    return jnp.where(rows == 0, 0.0, pltpu.roll(a, 1, 0))


def plane_after(a):
    last = a.shape[0] - 1
    rows = lax.broadcasted_iota(jnp.int32, a.shape, 0)
    return jnp.where(rows == last, 0.0, pltpu.roll(a, last, 0))


def fetch_sources(refs, held, sems):
    copies = [pltpu.make_async_copy(src, dst, sems.at[i]) for i, (src, dst) in enumerate(zip(refs, held))]
    for copy in copies:
        copy.start()
    return copies


def plane_kernel(n, m, y, got_a, got_b, edge_a, edge_b, v_in, s_in, raw, coef_in, out_a, out_b, vb, sb, coef, below, above):
    del v_in, s_in, coef_in
    horiz, vert = lax.axis_index("horiz"), lax.axis_index("vert")
    odd = vert % 2 == 1
    has_below = jnp.where(vert > 0, 1.0, 0.0)
    has_above = jnp.where(vert < lax.axis_size("vert") - 1, 1.0, 0.0)
    for t in range(MSG // 8):
        at = pl.ds(8 * t, 8)
        a, b = got_a[at, :], got_b[at, :]
        below[at, :] = has_below * jnp.where(odd, a, b)
        above[at, :] = has_above * jnp.where(odd, b, a)
    lowest, first, second = PAD - 1, PAD + m, PAD + m + 1
    base = 12 * n
    for c in range(4):
        for r, side in ((lowest, below), (first, above)):
            value = side[pl.ds(base + c, 1), :]
            coef[c, pl.ds(r, 1), :] = value * coef[c, pl.ds(r, 1), :] if c == 3 else value
    coef[0, pl.ds(second, 1), :] = above[pl.ds(base + 4, 1), :]

    def cs(c, r, size):
        return coef[c, pl.ds(r, size), :]

    s_line, v_line, s2, v2 = lines(n, m, y, vb, sb)
    low = [below[pl.ds(f * n, n), :] for f in range(9)]
    high = [above[pl.ds(f * n, n), :] for f in range(12)]
    own = [None] * 6
    for f in top:
        at = pl.ds(f * n, n)
        own[f] = jnp.where(odd, edge_b[at, :], edge_a[at, :])

    def beyond(f, dx, dz):
        if dz:
            return own[f]
        return plane_before(high[f]) if dx else high[f]

    v_high = velocity_tile(memo(beyond), lambda k: high[6 + k], cs(0, first, 1), cs(1, first, 1))
    change = [-cs(0, PAD, 1) * low[top[k]] for k in range(3)]
    v_low = [v2[v_line(k, PAD), :] + change[k] for k in range(3)]
    for k in range(3):
        v2[v_line(k, first), :] = v_high[k]
        v2[v_line(k, PAD), :] = v_low[k]

    def add_terms(r, grads, wanted, start=None):
        terms = stress_terms(grads, cs(2, r, 1), cs(3, r, 1), wanted)
        for c in wanted:
            line = s_line(c, r)
            old = s2[line, :]
            s2[line, :] = old + terms[c] if start is None else old + (start[c] + terms[c])

    def across(v):
        return [plane_after(v) - v, None, fore_lane(v)]

    def grads_of(values, next_values):
        out = []
        for v, after in zip(values, next_values):
            grad = across(v)
            grad[1] = -v if after is None else after - v
            out.append(grad)
        return out

    add_terms(lowest, grads_of(low[6:9], v_low), top, low)
    add_terms(PAD, grads_of(change, [None] * 3), range(6))
    add_terms(first, grads_of(v_high, high[9:12]), range(6), high)
    rl, rm = cs(2, first - 1, 1), cs(3, first - 1, 1)
    spread = rl * v_high[1]
    for c, term in ((0, spread), (1, spread + 2.0 * rm * v_high[1]), (2, spread), (3, rm * v_high[0]), (5, rm * v_high[2])):
        line = s_line(c, first - 1)
        s2[line, :] = s2[line, :] + term

    even = horiz % 2 == 0
    tiles = [(PAD + 8 * t, 8) for t in range(m // 8)]
    tail = 6 * m

    def put(at, size, to_right, to_left):
        out_a[pl.ds(at, size), :] = jnp.where(even, to_right, to_left)
        out_b[pl.ds(at, size), :] = jnp.where(even, to_left, to_right)

    for r, size in tiles:
        new = velocity_tile(
            memo(lambda f, dx, dz: 0.0 if dx else sb[f, 1, pl.ds(r + dz, size), :]),
            lambda k: vb[k, 1, pl.ds(r, size), :],
            cs(0, r, size),
            cs(1, r, size),
        )
        for c, f in enumerate(front):
            put(c * m + r - PAD, size, raw[c, pl.ds(r - PAD, size), :], vb[c, 1, pl.ds(r, size), :])
            put((3 + c) * m + r - PAD, size, sb[f, n, pl.ds(r, size), :], new[c])
    for c, f in enumerate(front):
        last = f * n + n - 1
        before_low, before_first = below[pl.ds(last, 1), :], above[pl.ds(last, 1), :]
        put(tail + c, 1, before_low, below[pl.ds((6 + c) * n, 1), :])
        put(tail + 3 + c, 1, before_first, vb[c, 1, pl.ds(first, 1), :])
        before_second, after_first = above[pl.ds(base + 5 + c, 1), :], sb[f, n, pl.ds(first, 1), :]
        put(tail + 6 + c, 1, before_second, before_second)
        put(tail + 9 + c, 1, after_first, after_first)


def rest_kernel(n, m, y, v_in, s_in, coef, *refs):
    sources, (vb, sb, out_v, out_s), scratch = refs[:4], refs[4:8], refs[8:]
    sx, sz, sy, amp, near_x, near_z, near_y, near_amp, small, sems = scratch
    del v_in, s_in
    horiz, vert = lax.axis_index("horiz"), lax.axis_index("vert")
    fetched = fetch_sources(sources, (sx, sz, sy, amp), small)
    body = pl.ds(PAD, m)
    first = PAD + m
    tiles = [(PAD + 8 * t, 8) for t in range(m // 8)]

    def cs(c, r, size):
        return coef[c, pl.ds(r, size), :]

    s_line, v_line, s2, v2 = lines(n, m, y, vb, sb)

    def beyond(f, dx, dz):
        here = s2[s_line(f, first + dz), :]
        return plane_before(here) if dx else here

    new = velocity_tile(memo(beyond), lambda k: v2[v_line(k, first), :], cs(0, first, 1), cs(1, first, 1))
    for k in range(3):
        v2[v_line(k, first), :] = new[k]

    def move(x):
        for r, size in tiles:
            new = velocity_tile(
                memo(lambda f, dx, dz: sb[f, x + 1 + dx, pl.ds(r + dz, size), :]),
                lambda k: vb[k, x + 1, pl.ds(r, size), :],
                cs(0, r, size),
                cs(1, r, size),
            )
            for k in range(3):
                vb[k, x + 1, pl.ds(r, size), :] = new[k]

    def load(x):
        for r, size in tiles:
            g = strain(memo(lambda k, dx, dz: vb[k, x + 1 + dx, pl.ds(r + dz, size), :]))
            terms = stress_terms(g, cs(2, r, size), cs(3, r, size))
            for c in range(6):
                sb[c, x + 1, pl.ds(r, size), :] = sb[c, x + 1, pl.ds(r, size), :] + terms[c]

    for copy in fetched:
        copy.wait()
    found = jnp.int32(0)
    for i in range(sx.shape[0]):
        x, z = sx[i] - horiz * n, sz[i] - vert * m
        near_x[found], near_z[found], near_y[found], near_amp[found] = x, z, sy[i], amp[i]
        found = found + ((x >= 0) & (x < n) & (z >= 0) & (z < m)).astype(jnp.int32)

    def add_near(x_low, x_high):
        def add(j, carry):
            x, z = near_x[j], near_z[j]

            @pl.when((x >= x_low) & (x < x_high))
            def _():
                row = jnp.where(lane_of((1, y)) == near_y[j], courant * wavelet[1] * near_amp[j], 0.0)
                at = pl.ds(PAD + z, 1)
                for c in range(3):
                    sb[c, x + 1, at, :] = sb[c, x + 1, at, :] + row

            return carry

        lax.fori_loop(0, found, add, 0)

    def v_off(x):
        return pltpu.make_async_copy(vb.at[:, x + 1, body], out_v.at[:, x], sems.at[0, x])

    def s_off(x):
        return pltpu.make_async_copy(sb.at[:, x + 1, body], out_s.at[:, x], sems.at[1, x])

    def send(off, x, end):
        @pl.when((x >= 2) & (x < end))
        def _():
            off(x).start()

    def advance(g, carry):
        x = GROUP * g
        for p in range(GROUP):
            move(x + p)
        for p in range(GROUP):
            send(v_off, x + p, n - 2)
        for p in range(-1, GROUP - 1):
            load(x + p)
        add_near(x - 1, x + GROUP - 1)
        for p in range(-1, GROUP - 1):
            send(s_off, x + p, n - 1 - GROUP)
        return carry

    lax.fori_loop(0, n // GROUP, advance, 0)
    load(n - 1)
    add_near(n - 1, n)

    def finish(x, carry):
        v_off(x).wait()

        @pl.when(x < n - 1 - GROUP)
        def _():
            s_off(x).wait()

        return carry

    lax.fori_loop(2, n - 2, finish, 0)


def join_kernel(n, m, y, next_b, next_a, own_a, own_b, coef, vb, sb, v_in, s_in, v_out, s_out, *scratch):
    wa, da, ds, dv, dw, qb, db, es, ev, vn, v0, v1, s0, s1, sems = scratch
    del v_in, s_in
    horiz = lax.axis_index("horiz")
    even = horiz % 2 == 0
    has_left = jnp.where(horiz > 0, 1.0, 0.0)
    has_right = jnp.where(horiz < lax.axis_size("horiz") - 1, 1.0, 0.0)
    lowest, first, second = PAD - 1, PAD + m, PAD + m + 1
    tail = 6 * m
    tiles = [(PAD + 8 * t, 8) for t in range(m // 8)]

    def cs(c, r, size):
        return coef[c, pl.ds(r, size), :]

    pick = {"right": (next_a, next_b), "left": (next_b, next_a), "own right": (own_a, own_b), "own left": (own_b, own_a)}

    def rows_of(which, at, size):
        a, b = pick[which]
        return jnp.where(even, a[pl.ds(at, size), :], b[pl.ds(at, size), :])

    def msg(which, c, r, size):
        return rows_of(which, c * m + r - PAD, size)

    def end(which, at):
        return rows_of(which, tail + at, 1)

    for k in range(3):
        rows = [(r, size, msg("left", k, r, size)) for r, size in tiles]
        rows += [(r, 1, end("left", at + k)) for r, at in ((lowest, 0), (first, 3), (second, 6))]
        for r, size, value in rows:
            da[k, pl.ds(r, size), :] = -(has_left * cs(0, r, size)) * value
        rows = [(r, size, msg("left", 3 + k, r, size), msg("own left", k, r, size)) for r, size in tiles]
        rows += [(first, 1, end("left", 9 + k), end("own left", 3 + k))]
        for r, size, value, own in rows:
            gain = cs(3, r, size) if k else cs(2, r, size) + 2.0 * cs(3, r, size)
            wa[k, pl.ds(r, size), :] = has_left * (value + gain * (own + da[k, pl.ds(r, size), :]))
        rows = [(r, size, msg("own right", k, r, size), msg("right", k, r, size)) for r, size in tiles]
        rows += [(r, 1, end("own right", at + k), end("right", at + k)) for r, at in ((lowest, 0), (first, 3))]
        for r, size, value, other in rows:
            change = -(has_right * cs(0, r, size)) * value
            db[k, pl.ds(r, size), :] = change
            qb[k, pl.ds(r, size), :] = has_right * other + change

    def strain_of(buf, r, size, ahead=None):
        grads = []
        for i in range(3):
            here = buf[i, pl.ds(r, size), :]
            beyond = -here if ahead is None else ahead[i, pl.ds(r, size), :] - here
            grads.append([beyond, buf[i, pl.ds(r + 1, size), :] - here, fore_lane(here)])
        return grads

    for out, src, ends in ((ds, da, (lowest, first)), (es, db, (lowest,))):
        parts = [(r, size, range(6)) for r, size in tiles]
        parts += [(r, 1, top if r == lowest else range(6)) for r in ends]
        for r, size, wanted in parts:
            terms = stress_terms(strain_of(src, r, size), cs(2, r, size), cs(3, r, size), wanted)
            for c in wanted:
                out[c, pl.ds(r, size), :] = terms[c]

    for r, size in tiles + [(first, 1)]:
        rb, dq = cs(0, r, size), cs(1, r, size)
        for k in range(3):
            a, b, c = pair_table[k]
            here = ds[a, pl.ds(r, size), :]
            total = here - wa[k, pl.ds(r, size), :]
            total = total + (ds[b, pl.ds(r, size), :] - ds[b, pl.ds(r - 1, size), :])
            total = total + back_lane(ds[c, pl.ds(r, size), :])
            dv[k, pl.ds(r, size), :] = dq * da[k, pl.ds(r, size), :] + rb * total
            dw[k, pl.ds(r, size), :] = -rb * here

    def last_stress(c, r, size):
        q = qb[0 if c < 3 else c - 2, pl.ds(r, size), :]
        if c == 0:
            return (cs(2, r, size) + 2.0 * cs(3, r, size)) * q
        return (cs(2, r, size) if c < 3 else cs(3, r, size)) * q

    for r, size in tiles + [(first, 1)]:
        rb, dq = cs(0, r, size), cs(1, r, size)
        full = [last_stress(c, r, size) for c in range(5)]
        totals = [
            full[0] + (full[3] - last_stress(3, r - 1, size)) + back_lane(full[4]),
            full[3] + (full[1] - last_stress(1, r - 1, size)),
            full[4] + back_lane(full[2]),
        ]
        for k in range(3):
            ev[k, pl.ds(r, size), :] = rb * totals[k]
        if r == first:
            continue
        for k in range(3):
            a, b, c = pair_table[k]
            total = es[a, pl.ds(r, size), :] - (msg("own right", 3 + k, r, size) + full[a])
            total = total + (es[b, pl.ds(r, size), :] - es[b, pl.ds(r - 1, size), :])
            total = total + back_lane(es[c, pl.ds(r, size), :])
            change = dq * db[k, pl.ds(r, size), :] + rb * total
            vn[k, pl.ds(r, size), :] = has_right * (msg("right", 3 + k, r, size) + change)

    def put(buf, dst, x, i):
        copy = pltpu.make_async_copy(buf, dst.at[:, x], sems.at[i])
        copy.start()
        return copy

    rest = pltpu.make_async_copy(
        sb.at[:, pl.ds(n - GROUP, GROUP - 1), pl.ds(PAD, m)], s_out.at[:, pl.ds(n - 1 - GROUP, GROUP - 1)], sems.at[8]
    )
    rest.start()
    copies = [rest]
    for buf, x, change in ((v0.at[:, 0], 0, dv), (v0.at[:, 1], 1, dw), (v1.at[:, 0], n - 1, ev), (v1.at[:, 1], n - 2, None)):
        for r, size in tiles:
            out, at = pl.ds(r - PAD, size), pl.ds(r, size)
            for k in range(3):
                old = vb[k, x + 1, at, :]
                buf[k, out, :] = old if change is None else old + change[k, at, :]
        copies.append(put(buf, v_out, x, len(copies) - 1))
    for buf, x, src, ahead, more in (
        (s0.at[:, 0], 0, dv, dw, lambda c, r: ds[c, pl.ds(r, 8), :]),
        (s0.at[:, 1], 1, dw, None, None),
        (s1.at[:, 0], n - 1, ev, vn, lambda c, r: None if c == 5 else last_stress(c, r, 8)),
    ):
        for r, size in tiles:
            out, at = pl.ds(r - PAD, size), pl.ds(r, size)
            terms = stress_terms(strain_of(src, r, size, ahead), cs(2, r, size), cs(3, r, size))
            for c in range(6):
                extra = None if more is None else more(c, r)
                term = terms[c] if extra is None else terms[c] + extra
                buf[c, out, :] = sb[c, x + 1, at, :] + term
        copies.append(put(buf, s_out, x, len(copies) - 1))
    for r, size in tiles:
        out, at = pl.ds(r - PAD, size), pl.ds(r, size)
        rl, rm = cs(2, r, size), cs(3, r, size)
        e = [ev[k, at, :] for k in range(3)]
        spread = rl * e[0]
        for c, term in enumerate((spread + 2.0 * rm * e[0], spread, spread, rm * e[1], rm * e[2], None)):
            old = sb[c, n - 1, at, :]
            s1[c, 1, out, :] = old if term is None else old + term
    copies.append(put(s1.at[:, 1], s_out, n - 2, len(copies) - 1))
    for copy in copies:
        copy.wait()


def local(velocity, stress, index, table, split, source_x, source_z, source_y, amplitude):
    _, n, m, y = velocity.shape
    f32, i32 = jnp.float32, jnp.int32
    high = m + 16
    dma = pltpu.SemaphoreType.DMA
    sources = (source_x, source_z, source_y, amplitude)
    held = [pltpu.SMEM(a.shape, a.dtype) for a in sources]
    near = [pltpu.SMEM((a.shape[0] + 1,), a.dtype) for a in sources]
    table = table.T
    materials = [pltpu.SMEM((m,), i32), pltpu.SMEM(table.shape, f32)]

    def shape(*dims):
        return jax.ShapeDtypeStruct(dims, f32)

    def kept(*dims):
        return pltpu.VMEM(dims, f32)

    def outside(*dims):
        return pltpu.HBM(dims, f32)

    def room(mib):
        return pltpu.CompilerParams(vmem_limit_bytes=mib * 1024 * 1024)

    def cost(flops, moved):
        return pl.CostEstimate(flops=flops, bytes_accessed=moved, transcendentals=0)

    padded_v, padded_s = kept(3, n + 2, high, y), kept(6, n + 1, high, y)
    edge_a, edge_b, coef = pl.pallas_call(
        functools.partial(edge_kernel, n, m, y),
        out_shape=[kept(MSG, y)] * 2 + [kept(4, high, y)],
        in_specs=[HBM] * 4,
        out_specs=[VMEM] * 3,
        scratch_shapes=[pltpu.VMEM((9, n + 1, 8, y), f32)] * 2 + materials + [dma((6,))],
        compiler_params=room(EDGE_MIB),
        name="edge_levels",
    )(*[pltpu.with_memory_space_constraint(a, pltpu.HBM) for a in (velocity, stress, index, table)])
    got_a, got_b = swap(edge_a, 2, False), swap(edge_b, 2, True)
    split, edge_a = lax.optimization_barrier((split, edge_a))
    vb, sb, raw, coef = pl.pallas_call(
        functools.partial(load_kernel, n, m, y),
        out_shape=[padded_v, padded_s, kept(3, m, y), kept(4, high, y)],
        in_specs=[VMEM, VMEM, VMEM, SMEM] + [ANY] * 4,
        out_specs=[VMEM] * 4,
        input_output_aliases={2: 3},
        scratch_shapes=[*held, dma((4,))],
        compiler_params=room(LOAD_MIB),
        cost_estimate=cost(60 * n * m * y, 4 * 9 * n * m * y),
        name="load_block",
    )(*[pltpu.with_memory_space_constraint(a, pltpu.VMEM) for a in (velocity, stress)], coef, split, *sources)
    plane_a, plane_b, vb, sb, coef = pl.pallas_call(
        functools.partial(plane_kernel, n, m, y),
        out_shape=[kept(6 * m + 16, y)] * 2 + [padded_v, padded_s, kept(4, high, y)],
        in_specs=[VMEM] * 8,
        out_specs=[VMEM] * 5,
        input_output_aliases={4: 2, 5: 3, 7: 4},
        scratch_shapes=[pltpu.VMEM((MSG, y), f32)] * 2,
        compiler_params=room(SMALL_MIB),
        name="edge_planes",
    )(got_a, got_b, edge_a, edge_b, vb, sb, raw, coef)
    next_b = swap(plane_b, 1, True)
    next_a = swap(plane_a, 1, False)
    vb, sb, v_own, s_own = pl.pallas_call(
        functools.partial(rest_kernel, n, m, y),
        out_shape=[padded_v, padded_s, outside(*velocity.shape), outside(*stress.shape)],
        in_specs=[VMEM] * 3 + [ANY] * 4,
        out_specs=[VMEM, VMEM, HBM, HBM],
        input_output_aliases={0: 0, 1: 1},
        scratch_shapes=[*held, *near, dma((4,)), dma((2, n))],
        compiler_params=room(SMALL_MIB),
        cost_estimate=cost(60 * n * m * y, 4 * 9 * n * m * y),
        name="both_steps",
    )(vb, sb, coef, *sources)
    plane = pltpu.VMEM((3, high, y), f32)
    plane6 = pltpu.VMEM((6, high, y), f32)
    return pl.pallas_call(
        functools.partial(join_kernel, n, m, y),
        out_shape=[outside(*velocity.shape), outside(*stress.shape)],
        in_specs=[VMEM] * 7 + [HBM] * 2,
        out_specs=[HBM, HBM],
        input_output_aliases={7: 0, 8: 1},
        scratch_shapes=[plane, plane, plane6, plane, plane, plane, plane, plane6, plane, plane]
        + [pltpu.VMEM((3, 2, m, y), f32)] * 2
        + [pltpu.VMEM((6, 2, m, y), f32)] * 2
        + [dma((9,))],
        compiler_params=room(SMALL_MIB),
        name="join_neighbours",
    )(next_b, next_a, plane_a, plane_b, coef, vb, sb, v_own, s_own)


def solution(mesh):
    block = P("member", "horiz", "vert", None)
    return jax.shard_map(
        local,
        mesh=mesh,
        in_specs=(block, block, P("vert"), P(), P(), P(), P(), P(), P("member")),
        out_specs=(block, block),
        check_vma=False,
    )
```

```python
import functools

import jax
import jax.numpy as jnp
from jax import lax
from jax.experimental import pallas as pl
from jax.experimental.pallas import tpu as pltpu
from jax.sharding import PartitionSpec as P

courant = 0.2
wavelet = (1.0, -0.5)
pair_table = ((0, 3, 4), (3, 1, 5), (4, 5, 2))
front = (0, 3, 4)
top = (3, 1, 5)
PAD = 8
ANY = pl.BlockSpec(memory_space=pl.ANY)
HBM = pl.BlockSpec(memory_space=pltpu.HBM)
VMEM = pl.BlockSpec(memory_space=pltpu.VMEM)
SMEM = pl.BlockSpec(memory_space=pltpu.SMEM)


def swap_pairs(sizes, along, odd):
    members, rows, cols = sizes
    out = []
    for a in range(members):
        for i in range(rows):
            for j in range(cols):
                here = [a, i, j]
                there = [a, i, j]
                if not odd:
                    there[along] ^= 1
                elif 0 < here[along] < sizes[along] - 1:
                    there[along] += 1 if here[along] % 2 else -1
                else:
                    there[1 if along == 2 else 2 if members % 2 else 0] ^= 1
                out.append(tuple((p[0] * rows + p[1]) * cols + p[2] for p in (here, there)))
    return out


def swap(block, along, odd):
    axes = ("member", "horiz", "vert")
    return lax.ppermute(block, axes, swap_pairs([lax.axis_size(a) for a in axes], along, odd))


def lane_of(shape):
    return lax.broadcasted_iota(jnp.int32, shape, len(shape) - 1)


def back_lane(a):
    moved = pltpu.roll(a, 1, 1)
    return a - jnp.where(lane_of(a.shape) == 0, 0.0, moved)


def fore_lane(a):
    last = a.shape[-1] - 1
    moved = pltpu.roll(a, last, 1)
    return jnp.where(lane_of(a.shape) == last, 0.0, moved) - a


def velocity_tile(s_at, v_at, rb, dq):
    out = []
    for k in range(3):
        a, b, c = pair_table[k]
        total = (s_at(a, 0, 0) - s_at(a, -1, 0)) + (s_at(b, 0, 0) - s_at(b, 0, -1))
        total = total + back_lane(s_at(c, 0, 0))
        out.append(dq * v_at(k) + rb * total)
    return out


def strain(v_at):
    grads = []
    for i in range(3):
        here = v_at(i, 0, 0)
        grads.append([v_at(i, 1, 0) - here, v_at(i, 0, 1) - here, fore_lane(here)])
    return grads


def stress_terms(g, rl, rm, wanted=range(6)):
    out = {}
    if any(c < 3 for c in wanted):
        spread = rl * (g[0][0] + g[1][1] + g[2][2])
    for c in wanted:
        if c < 3:
            out[c] = spread + 2.0 * rm * g[c][c]
        else:
            i, j = ((0, 1), (0, 2), (1, 2))[c - 3]
            out[c] = rm * (g[i][j] + g[j][i])
    return out


def memo(fn):
    seen = {}

    def call(*key):
        if key not in seen:
            seen[key] = fn(*key)
        return seen[key]

    return call


MSG = 200


def level_scalars(index_ref, table_ref, z):
    kind = index_ref[z]
    return (
        courant * table_ref[0, kind],
        1.0 - courant * table_ref[3, kind],
        courant * table_ref[1, kind],
        courant * table_ref[2, kind],
    )


def edge_kernel(
    n, m, y, v_ref, s_ref, index, table, out_a, out_b, coef, low, high, index_ref, table_ref, sems
):
    vert = lax.axis_index("vert")
    odd = vert % 2 == 1
    copies = []
    for at, (buf, start) in enumerate(((low, 0), (high, m - 8))):
        copies.append(
            pltpu.make_async_copy(s_ref.at[:, :, pl.ds(start, 8), :], buf.at[pl.ds(0, 6), pl.ds(1, n)], sems.at[2 * at])
        )
        copies.append(
            pltpu.make_async_copy(
                v_ref.at[:, :, pl.ds(start, 8), :], buf.at[pl.ds(6, 3), pl.ds(1, n)], sems.at[2 * at + 1]
            )
        )
    scalars = [
        pltpu.make_async_copy(src, dst, sems.at[4 + i])
        for i, (src, dst) in enumerate(((index, index_ref), (table, table_ref)))
    ]
    for copy in scalars + copies:
        copy.start()
    for buf in (low, high):
        for f in front:
            buf[f, 0] = jnp.zeros((8, y), jnp.float32)
    for copy in scalars:
        copy.wait()
    at_first = level_scalars(index_ref, table_ref, 0)
    at_second = level_scalars(index_ref, table_ref, 1)
    at_last = level_scalars(index_ref, table_ref, m - 1)

    def level(z, carry):
        for c, value in enumerate(level_scalars(index_ref, table_ref, z)):
            coef[c, pl.ds(PAD + z, 1), :] = jnp.full((1, y), value, jnp.float32)
        return carry

    lax.fori_loop(0, m, level, 0, unroll=8)
    for copy in copies:
        copy.wait()
    low2 = low.reshape(9 * (n + 2) * 8, y)
    high2 = high.reshape(9 * (n + 2) * 8, y)

    def row(buf, f, z, dx=0):
        return buf[pl.Slice((f * (n + 2) + 1 + dx) * 8 + z, n, 8), :]

    def moved(buf, z, scal):
        return velocity_tile(
            memo(lambda f, dx, dz: row(buf, f, z + dz, dx)), lambda k: row(buf, 6 + k, z), scal[0], scal[1]
        )

    up = [row(high2, f, 7) for f in range(6)] + moved(high2, 7, at_last)
    down = [row(low2, f, 0) for f in range(9)] + moved(low2, 1, at_second)

    def put(at, rows, up_value, down_value):
        out_a[pl.ds(at, rows), :] = jnp.where(odd, down_value, up_value)
        out_b[pl.ds(at, rows), :] = jnp.where(odd, up_value, down_value)

    for f in range(12):
        put(f * n, n, up[f] if f < 9 else down[f], down[f])
    base = 12 * n
    for c in range(4):
        splat = [jnp.full((1, y), a[c], jnp.float32) for a in (at_last, at_first)]
        put(base + c, 1, *splat)
    ahead = jnp.full((1, y), at_second[0], jnp.float32)
    put(base + 4, 1, ahead, ahead)
    for c, f in enumerate(front):
        corner = low[f, n, pl.ds(1, 1), :]
        put(base + 5 + c, 1, corner, corner)


EDGE_MIB, LOAD_MIB, SMALL_MIB = 16, 16, 16
GROUP = 8


def load_kernel(n, m, y, v_ref, s_ref, coef_in, split, *refs):
    sources, (vb, sb, raw, coef), scratch = refs[:4], refs[4:8], refs[8:]
    sx, sz, sy, amp, small = scratch
    del coef_in
    fetched = fetch_sources(sources, (sx, sz, sy, amp), small)
    for f in front:
        sb[f, 0] = jnp.zeros((m + 16, y), jnp.float32)
    for k in range(3):
        vb[k, n + 1] = jnp.zeros((m + 16, y), jnp.float32)
    lowest, first = PAD - 1, PAD + m
    s_line, v_line, s2, v2 = lines(n, m, y, vb, sb)
    zero = jnp.zeros((n, y), jnp.float32)
    for f in range(6):
        s2[s_line(f, lowest), :] = zero
        s2[s_line(f, first), :] = zero
    for k in range(3):
        v2[v_line(k, first), :] = zero
    coef[3, pl.ds(lowest, 1), :] = jnp.ones((1, y), jnp.float32)
    coef[3, pl.ds(first, 1), :] = jnp.ones((1, y), jnp.float32)
    start = split[0] - lax.axis_index("vert") * m
    tiles = [PAD + 8 * t for t in range(m // 8)]
    for r, size in [(r, 8) for r in tiles] + [(lowest, 1), (first, 1)]:
        level = r - PAD + lax.broadcasted_iota(jnp.int32, (size, y), 0)
        at = pl.ds(r, size)
        coef[3, at, :] = jnp.where(level >= start, coef[3, at, :], 0.0)

    def cs(c, r):
        return coef[c, pl.ds(r, 8), :]

    def move(x, first_group=False):
        for r in tiles:
            rb, dq = cs(0, r), cs(1, r)

            def stress_of(f, p, dz):
                if p < 0 and first_group:
                    return 0.0
                if dz and r == PAD:
                    return plane_before(s_ref[f, x + p, pl.ds(0, 8), :])
                return s_ref[f, x + p, pl.ds(r - PAD + dz, 8), :]

            stress_of = memo(stress_of)
            for p in range(GROUP):
                new = velocity_tile(
                    lambda f, dx, dz: stress_of(f, p + dx, dz), lambda k: v_ref[k, x + p, pl.ds(r - PAD, 8), :], rb, dq
                )
                for k in range(3):
                    vb[k, x + p + 1, pl.ds(r, 8), :] = new[k]

    def load(g, carry):
        x = GROUP * g
        for r in tiles:
            rl, rm = cs(2, r), cs(3, r)
            speed_of = memo(lambda k, p, dz: vb[k, x + p + 1, pl.ds(r + dz, 8), :])
            for p in range(GROUP):
                terms = stress_terms(strain(lambda k, dx, dz: speed_of(k, p + dx, dz)), rl, rm)
                for c in range(6):
                    sb[c, x + p + 1, pl.ds(r, 8), :] = s_ref[c, x + p, pl.ds(r - PAD, 8), :] + terms[c]
        return carry

    move(0, True)
    lax.fori_loop(1, n // GROUP, lambda g, carry: (move(GROUP * g), carry)[1], 0)
    lax.fori_loop(0, n // GROUP, load, 0)
    for c, f in enumerate(front):
        raw[c] = s_ref[f, n - 1]
    for copy in fetched:
        copy.wait()
    x_at, z_at = lax.axis_index("horiz") * n, lax.axis_index("vert") * m

    def add(i, carry):
        x, z = sx[i] - x_at, sz[i] - z_at

        @pl.when((x >= 0) & (x < n) & (z >= -1) & (z <= m))
        def _():
            row = jnp.where(lane_of((1, y)) == sy[i], courant * wavelet[0] * amp[i], 0.0)
            at = pl.ds(PAD + z, 1)
            for c in range(3):
                sb[c, x + 1, at, :] = sb[c, x + 1, at, :] + row

        return carry

    lax.fori_loop(0, sx.shape[0], add, 0)


def lines(n, m, y, vb, sb):
    high = m + 16

    def s_line(f, r):
        return pl.Slice((f * (n + 2) + 1) * high + r, n, high)

    def v_line(k, r):
        return pl.Slice((k * (n + 2) + 1) * high + r, n, high)

    return s_line, v_line, sb.reshape(6 * (n + 2) * high, y), vb.reshape(3 * (n + 2) * high, y)


def plane_before(a):
    rows = lax.broadcasted_iota(jnp.int32, a.shape, 0)
    return jnp.where(rows == 0, 0.0, pltpu.roll(a, 1, 0))


def plane_after(a):
    last = a.shape[0] - 1
    rows = lax.broadcasted_iota(jnp.int32, a.shape, 0)
    return jnp.where(rows == last, 0.0, pltpu.roll(a, last, 0))


def fetch_sources(refs, held, sems):
    copies = [pltpu.make_async_copy(src, dst, sems.at[i]) for i, (src, dst) in enumerate(zip(refs, held))]
    for copy in copies:
        copy.start()
    return copies


def plane_kernel(n, m, y, got_a, got_b, edge_a, edge_b, v_in, s_in, raw, coef_in, out_a, out_b, vb, sb, coef, below, above):
    del v_in, s_in, coef_in
    horiz, vert = lax.axis_index("horiz"), lax.axis_index("vert")
    odd = vert % 2 == 1
    has_below = jnp.where(vert > 0, 1.0, 0.0)
    has_above = jnp.where(vert < lax.axis_size("vert") - 1, 1.0, 0.0)
    for t in range(MSG // 8):
        at = pl.ds(8 * t, 8)
        a, b = got_a[at, :], got_b[at, :]
        below[at, :] = has_below * jnp.where(odd, a, b)
        above[at, :] = has_above * jnp.where(odd, b, a)
    lowest, first, second = PAD - 1, PAD + m, PAD + m + 1
    base = 12 * n
    for c in range(4):
        for r, side in ((lowest, below), (first, above)):
            value = side[pl.ds(base + c, 1), :]
            coef[c, pl.ds(r, 1), :] = value * coef[c, pl.ds(r, 1), :] if c == 3 else value
    coef[0, pl.ds(second, 1), :] = above[pl.ds(base + 4, 1), :]

    def cs(c, r, size):
        return coef[c, pl.ds(r, size), :]

    s_line, v_line, s2, v2 = lines(n, m, y, vb, sb)
    low = [below[pl.ds(f * n, n), :] for f in range(9)]
    high = [above[pl.ds(f * n, n), :] for f in range(12)]
    own = [None] * 6
    for f in top:
        at = pl.ds(f * n, n)
        own[f] = jnp.where(odd, edge_b[at, :], edge_a[at, :])

    def beyond(f, dx, dz):
        if dz:
            return own[f]
        return plane_before(high[f]) if dx else high[f]

    v_high = velocity_tile(memo(beyond), lambda k: high[6 + k], cs(0, first, 1), cs(1, first, 1))
    change = [-cs(0, PAD, 1) * low[top[k]] for k in range(3)]
    v_low = [v2[v_line(k, PAD), :] + change[k] for k in range(3)]
    for k in range(3):
        v2[v_line(k, first), :] = v_high[k]
        v2[v_line(k, PAD), :] = v_low[k]

    def add_terms(r, grads, wanted, start=None):
        terms = stress_terms(grads, cs(2, r, 1), cs(3, r, 1), wanted)
        for c in wanted:
            line = s_line(c, r)
            old = s2[line, :]
            s2[line, :] = old + terms[c] if start is None else old + (start[c] + terms[c])

    def across(v):
        return [plane_after(v) - v, None, fore_lane(v)]

    def grads_of(values, next_values):
        out = []
        for v, after in zip(values, next_values):
            grad = across(v)
            grad[1] = -v if after is None else after - v
            out.append(grad)
        return out

    add_terms(lowest, grads_of(low[6:9], v_low), top, low)
    add_terms(PAD, grads_of(change, [None] * 3), range(6))
    add_terms(first, grads_of(v_high, high[9:12]), range(6), high)
    rl, rm = cs(2, first - 1, 1), cs(3, first - 1, 1)
    spread = rl * v_high[1]
    for c, term in ((0, spread), (1, spread + 2.0 * rm * v_high[1]), (2, spread), (3, rm * v_high[0]), (5, rm * v_high[2])):
        line = s_line(c, first - 1)
        s2[line, :] = s2[line, :] + term

    even = horiz % 2 == 0
    tiles = [(PAD + 8 * t, 8) for t in range(m // 8)]
    tail = 6 * m

    def put(at, size, to_right, to_left):
        out_a[pl.ds(at, size), :] = jnp.where(even, to_right, to_left)
        out_b[pl.ds(at, size), :] = jnp.where(even, to_left, to_right)

    for r, size in tiles:
        new = velocity_tile(
            memo(lambda f, dx, dz: 0.0 if dx else sb[f, 1, pl.ds(r + dz, size), :]),
            lambda k: vb[k, 1, pl.ds(r, size), :],
            cs(0, r, size),
            cs(1, r, size),
        )
        for c, f in enumerate(front):
            put(c * m + r - PAD, size, raw[c, pl.ds(r - PAD, size), :], vb[c, 1, pl.ds(r, size), :])
            put((3 + c) * m + r - PAD, size, sb[f, n, pl.ds(r, size), :], new[c])
    for c, f in enumerate(front):
        last = f * n + n - 1
        before_low, before_first = below[pl.ds(last, 1), :], above[pl.ds(last, 1), :]
        put(tail + c, 1, before_low, below[pl.ds((6 + c) * n, 1), :])
        put(tail + 3 + c, 1, before_first, vb[c, 1, pl.ds(first, 1), :])
        before_second, after_first = above[pl.ds(base + 5 + c, 1), :], sb[f, n, pl.ds(first, 1), :]
        put(tail + 6 + c, 1, before_second, before_second)
        put(tail + 9 + c, 1, after_first, after_first)


def rest_kernel(n, m, y, v_in, s_in, coef, *refs):
    sources, (vb, sb, out_v, out_s), scratch = refs[:4], refs[4:8], refs[8:]
    sx, sz, sy, amp, near_x, near_z, near_y, near_amp, small, sems = scratch
    del v_in, s_in
    horiz, vert = lax.axis_index("horiz"), lax.axis_index("vert")
    fetched = fetch_sources(sources, (sx, sz, sy, amp), small)
    body = pl.ds(PAD, m)
    first = PAD + m
    tiles = [(PAD + 8 * t, 8) for t in range(m // 8)]

    def cs(c, r, size):
        return coef[c, pl.ds(r, size), :]

    s_line, v_line, s2, v2 = lines(n, m, y, vb, sb)

    def beyond(f, dx, dz):
        here = s2[s_line(f, first + dz), :]
        return plane_before(here) if dx else here

    new = velocity_tile(memo(beyond), lambda k: v2[v_line(k, first), :], cs(0, first, 1), cs(1, first, 1))
    for k in range(3):
        v2[v_line(k, first), :] = new[k]

    def move(x, planes):
        for r, size in tiles:
            rb, dq = cs(0, r, size), cs(1, r, size)
            stress_of = memo(lambda f, p, dz: sb[f, x + p + 1, pl.ds(r + dz, size), :])
            for p in range(planes):
                new = velocity_tile(
                    lambda f, dx, dz: stress_of(f, p + dx, dz), lambda k: vb[k, x + p + 1, pl.ds(r, size), :], rb, dq
                )
                for k in range(3):
                    vb[k, x + p + 1, pl.ds(r, size), :] = new[k]

    def load(x, planes):
        for r, size in tiles:
            rl, rm = cs(2, r, size), cs(3, r, size)
            speed_of = memo(lambda k, p, dz: vb[k, x + p + 1, pl.ds(r + dz, size), :])
            for p in range(planes):
                terms = stress_terms(strain(lambda k, dx, dz: speed_of(k, p + dx, dz)), rl, rm)
                for c in range(6):
                    sb[c, x + p + 1, pl.ds(r, size), :] = sb[c, x + p + 1, pl.ds(r, size), :] + terms[c]

    for copy in fetched:
        copy.wait()
    found = jnp.int32(0)
    for i in range(sx.shape[0]):
        x, z = sx[i] - horiz * n, sz[i] - vert * m
        near_x[found], near_z[found], near_y[found], near_amp[found] = x, z, sy[i], amp[i]
        found = found + ((x >= 0) & (x < n) & (z >= 0) & (z < m)).astype(jnp.int32)

    def add_near(x_low, x_high):
        def add(j, carry):
            x, z = near_x[j], near_z[j]

            @pl.when((x >= x_low) & (x < x_high))
            def _():
                row = jnp.where(lane_of((1, y)) == near_y[j], courant * wavelet[1] * near_amp[j], 0.0)
                at = pl.ds(PAD + z, 1)
                for c in range(3):
                    sb[c, x + 1, at, :] = sb[c, x + 1, at, :] + row

            return carry

        lax.fori_loop(0, found, add, 0)

    def v_off(x):
        return pltpu.make_async_copy(vb.at[:, x + 1, body], out_v.at[:, x], sems.at[0, x])

    def s_off(x):
        return pltpu.make_async_copy(sb.at[:, x + 1, body], out_s.at[:, x], sems.at[1, x])

    def send(off, x, end):
        @pl.when((x >= 2) & (x < end))
        def _():
            off(x).start()

    def advance(x, planes):
        move(x, planes)
        for p in range(planes):
            send(v_off, x + p, n - 2)
        load(x - 1, planes)
        add_near(x - 1, x + planes - 1)
        for p in range(-1, planes - 1):
            send(s_off, x + p, n - 3)

    lax.fori_loop(0, n // GROUP - 1, lambda g, carry: (advance(GROUP * g, GROUP), carry)[1], 0)
    for x in range(n - GROUP, n, 2):
        advance(x, 2)
    load(n - 1, 1)
    add_near(n - 1, n)

    def finish(x, carry):
        v_off(x).wait()

        @pl.when(x < n - 3)
        def _():
            s_off(x).wait()

        return carry

    lax.fori_loop(2, n - 2, finish, 0)


def join_kernel(n, m, y, next_b, next_a, own_a, own_b, coef, vb, sb, v_in, s_in, v_out, s_out, *scratch):
    wa, da, ds, dv, dw, qb, db, es, ev, vn, v0, v1, s0, s1, sems = scratch
    del v_in, s_in
    horiz = lax.axis_index("horiz")
    even = horiz % 2 == 0
    has_left = jnp.where(horiz > 0, 1.0, 0.0)
    has_right = jnp.where(horiz < lax.axis_size("horiz") - 1, 1.0, 0.0)
    lowest, first, second = PAD - 1, PAD + m, PAD + m + 1
    tail = 6 * m
    tiles = [(PAD + 8 * t, 8) for t in range(m // 8)]

    def cs(c, r, size):
        return coef[c, pl.ds(r, size), :]

    pick = {"right": (next_a, next_b), "left": (next_b, next_a), "own right": (own_a, own_b), "own left": (own_b, own_a)}

    def rows_of(which, at, size):
        a, b = pick[which]
        return jnp.where(even, a[pl.ds(at, size), :], b[pl.ds(at, size), :])

    def msg(which, c, r, size):
        return rows_of(which, c * m + r - PAD, size)

    def end(which, at):
        return rows_of(which, tail + at, 1)

    for k in range(3):
        rows = [(r, size, msg("left", k, r, size)) for r, size in tiles]
        rows += [(r, 1, end("left", at + k)) for r, at in ((lowest, 0), (first, 3), (second, 6))]
        for r, size, value in rows:
            da[k, pl.ds(r, size), :] = -(has_left * cs(0, r, size)) * value
        rows = [(r, size, msg("left", 3 + k, r, size), msg("own left", k, r, size)) for r, size in tiles]
        rows += [(first, 1, end("left", 9 + k), end("own left", 3 + k))]
        for r, size, value, own in rows:
            gain = cs(3, r, size) if k else cs(2, r, size) + 2.0 * cs(3, r, size)
            wa[k, pl.ds(r, size), :] = has_left * (value + gain * (own + da[k, pl.ds(r, size), :]))
        rows = [(r, size, msg("own right", k, r, size), msg("right", k, r, size)) for r, size in tiles]
        rows += [(r, 1, end("own right", at + k), end("right", at + k)) for r, at in ((lowest, 0), (first, 3))]
        for r, size, value, other in rows:
            change = -(has_right * cs(0, r, size)) * value
            db[k, pl.ds(r, size), :] = change
            qb[k, pl.ds(r, size), :] = has_right * other + change

    def strain_of(buf, r, size, ahead=None):
        grads = []
        for i in range(3):
            here = buf[i, pl.ds(r, size), :]
            beyond = -here if ahead is None else ahead[i, pl.ds(r, size), :] - here
            grads.append([beyond, buf[i, pl.ds(r + 1, size), :] - here, fore_lane(here)])
        return grads

    for out, src, ends in ((ds, da, (lowest, first)), (es, db, (lowest,))):
        parts = [(r, size, range(6)) for r, size in tiles]
        parts += [(r, 1, top if r == lowest else range(6)) for r in ends]
        for r, size, wanted in parts:
            terms = stress_terms(strain_of(src, r, size), cs(2, r, size), cs(3, r, size), wanted)
            for c in wanted:
                out[c, pl.ds(r, size), :] = terms[c]

    for r, size in tiles + [(first, 1)]:
        rb, dq = cs(0, r, size), cs(1, r, size)
        for k in range(3):
            a, b, c = pair_table[k]
            here = ds[a, pl.ds(r, size), :]
            total = here - wa[k, pl.ds(r, size), :]
            total = total + (ds[b, pl.ds(r, size), :] - ds[b, pl.ds(r - 1, size), :])
            total = total + back_lane(ds[c, pl.ds(r, size), :])
            dv[k, pl.ds(r, size), :] = dq * da[k, pl.ds(r, size), :] + rb * total
            dw[k, pl.ds(r, size), :] = -rb * here

    def last_stress(c, r, size):
        q = qb[0 if c < 3 else c - 2, pl.ds(r, size), :]
        if c == 0:
            return (cs(2, r, size) + 2.0 * cs(3, r, size)) * q
        return (cs(2, r, size) if c < 3 else cs(3, r, size)) * q

    for r, size in tiles + [(first, 1)]:
        rb, dq = cs(0, r, size), cs(1, r, size)
        full = [last_stress(c, r, size) for c in range(5)]
        totals = [
            full[0] + (full[3] - last_stress(3, r - 1, size)) + back_lane(full[4]),
            full[3] + (full[1] - last_stress(1, r - 1, size)),
            full[4] + back_lane(full[2]),
        ]
        for k in range(3):
            ev[k, pl.ds(r, size), :] = rb * totals[k]
        if r == first:
            continue
        for k in range(3):
            a, b, c = pair_table[k]
            total = es[a, pl.ds(r, size), :] - (msg("own right", 3 + k, r, size) + full[a])
            total = total + (es[b, pl.ds(r, size), :] - es[b, pl.ds(r - 1, size), :])
            total = total + back_lane(es[c, pl.ds(r, size), :])
            change = dq * db[k, pl.ds(r, size), :] + rb * total
            vn[k, pl.ds(r, size), :] = has_right * (msg("right", 3 + k, r, size) + change)

    def put(buf, dst, x, i):
        copy = pltpu.make_async_copy(buf, dst.at[:, x], sems.at[i])
        copy.start()
        return copy

    body = pl.ds(PAD, m)
    copies = [
        pltpu.make_async_copy(sb.at[:, n - 2, body], s_out.at[:, n - 3], sems.at[7]),
        pltpu.make_async_copy(vb.at[:, n - 1, body], v_out.at[:, n - 2], sems.at[8]),
    ]
    for copy in copies:
        copy.start()
    for buf, x, change in ((v0.at[:, 0], 0, dv), (v0.at[:, 1], 1, dw), (v1.at[:, 0], n - 1, ev)):
        for r, size in tiles:
            out, at = pl.ds(r - PAD, size), pl.ds(r, size)
            for k in range(3):
                buf[k, out, :] = vb[k, x + 1, at, :] + change[k, at, :]
        copies.append(put(buf, v_out, x, len(copies) - 2))
    for buf, x, src, ahead, more in (
        (s0.at[:, 0], 0, dv, dw, lambda c, r: ds[c, pl.ds(r, 8), :]),
        (s0.at[:, 1], 1, dw, None, None),
        (s1.at[:, 0], n - 1, ev, vn, lambda c, r: None if c == 5 else last_stress(c, r, 8)),
    ):
        for r, size in tiles:
            out, at = pl.ds(r - PAD, size), pl.ds(r, size)
            terms = stress_terms(strain_of(src, r, size, ahead), cs(2, r, size), cs(3, r, size))
            for c in range(6):
                extra = None if more is None else more(c, r)
                term = terms[c] if extra is None else terms[c] + extra
                buf[c, out, :] = sb[c, x + 1, at, :] + term
        copies.append(put(buf, s_out, x, len(copies) - 2))
    for r, size in tiles:
        out, at = pl.ds(r - PAD, size), pl.ds(r, size)
        rl, rm = cs(2, r, size), cs(3, r, size)
        e = [ev[k, at, :] for k in range(3)]
        spread = rl * e[0]
        for c, term in enumerate((spread + 2.0 * rm * e[0], spread, spread, rm * e[1], rm * e[2], None)):
            old = sb[c, n - 1, at, :]
            s1[c, 1, out, :] = old if term is None else old + term
    copies.append(put(s1.at[:, 1], s_out, n - 2, len(copies) - 2))
    for copy in copies:
        copy.wait()


def local(velocity, stress, index, table, split, source_x, source_z, source_y, amplitude):
    _, n, m, y = velocity.shape
    f32, i32 = jnp.float32, jnp.int32
    high = m + 16
    dma = pltpu.SemaphoreType.DMA
    sources = (source_x, source_z, source_y, amplitude)
    held = [pltpu.SMEM(a.shape, a.dtype) for a in sources]
    near = [pltpu.SMEM((a.shape[0] + 1,), a.dtype) for a in sources]
    table = table.T
    materials = [pltpu.SMEM((m,), i32), pltpu.SMEM(table.shape, f32)]

    def shape(*dims):
        return jax.ShapeDtypeStruct(dims, f32)

    def kept(*dims):
        return pltpu.VMEM(dims, f32)

    def outside(*dims):
        return pltpu.HBM(dims, f32)

    def room(mib):
        return pltpu.CompilerParams(vmem_limit_bytes=mib * 1024 * 1024)

    def cost(flops, moved):
        return pl.CostEstimate(flops=flops, bytes_accessed=moved, transcendentals=0)

    padded_v, padded_s = kept(3, n + 2, high, y), kept(6, n + 2, high, y)
    edge_a, edge_b, coef = pl.pallas_call(
        functools.partial(edge_kernel, n, m, y),
        out_shape=[kept(MSG, y)] * 2 + [kept(4, high, y)],
        in_specs=[HBM] * 4,
        out_specs=[VMEM] * 3,
        scratch_shapes=[pltpu.VMEM((9, n + 2, 8, y), f32)] * 2 + materials + [dma((6,))],
        compiler_params=room(EDGE_MIB),
        name="edge_levels",
    )(*[pltpu.with_memory_space_constraint(a, pltpu.HBM) for a in (velocity, stress, index, table)])
    got_a, got_b = swap(edge_a, 2, False), swap(edge_b, 2, True)
    split, edge_a = lax.optimization_barrier((split, edge_a))
    vb, sb, raw, coef = pl.pallas_call(
        functools.partial(load_kernel, n, m, y),
        out_shape=[padded_v, padded_s, kept(3, m, y), kept(4, high, y)],
        in_specs=[VMEM, VMEM, VMEM, SMEM] + [ANY] * 4,
        out_specs=[VMEM] * 4,
        input_output_aliases={2: 3},
        scratch_shapes=[*held, dma((4,))],
        compiler_params=room(LOAD_MIB),
        cost_estimate=cost(60 * n * m * y, 4 * 9 * n * m * y),
        name="load_block",
    )(*[pltpu.with_memory_space_constraint(a, pltpu.VMEM) for a in (velocity, stress)], coef, split, *sources)
    plane_a, plane_b, vb, sb, coef = pl.pallas_call(
        functools.partial(plane_kernel, n, m, y),
        out_shape=[kept(6 * m + 16, y)] * 2 + [padded_v, padded_s, kept(4, high, y)],
        in_specs=[VMEM] * 8,
        out_specs=[VMEM] * 5,
        input_output_aliases={4: 2, 5: 3, 7: 4},
        scratch_shapes=[pltpu.VMEM((MSG, y), f32)] * 2,
        compiler_params=room(SMALL_MIB),
        name="edge_planes",
    )(got_a, got_b, edge_a, edge_b, vb, sb, raw, coef)
    next_b = swap(plane_b, 1, True)
    next_a = swap(plane_a, 1, False)
    vb, sb, v_own, s_own = pl.pallas_call(
        functools.partial(rest_kernel, n, m, y),
        out_shape=[padded_v, padded_s, outside(*velocity.shape), outside(*stress.shape)],
        in_specs=[VMEM] * 3 + [ANY] * 4,
        out_specs=[VMEM, VMEM, HBM, HBM],
        input_output_aliases={0: 0, 1: 1},
        scratch_shapes=[*held, *near, dma((4,)), dma((2, n))],
        compiler_params=room(SMALL_MIB),
        cost_estimate=cost(60 * n * m * y, 4 * 9 * n * m * y),
        name="both_steps",
    )(vb, sb, coef, *sources)
    plane = pltpu.VMEM((3, high, y), f32)
    plane6 = pltpu.VMEM((6, high, y), f32)
    return pl.pallas_call(
        functools.partial(join_kernel, n, m, y),
        out_shape=[outside(*velocity.shape), outside(*stress.shape)],
        in_specs=[VMEM] * 7 + [HBM] * 2,
        out_specs=[HBM, HBM],
        input_output_aliases={7: 0, 8: 1},
        scratch_shapes=[plane, plane, plane6, plane, plane, plane, plane, plane6, plane, plane]
        + [pltpu.VMEM((3, 2, m, y), f32), pltpu.VMEM((3, 1, m, y), f32)]
        + [pltpu.VMEM((6, 2, m, y), f32)] * 2
        + [dma((9,))],
        compiler_params=room(SMALL_MIB),
        name="join_neighbours",
    )(next_b, next_a, plane_a, plane_b, coef, vb, sb, v_own, s_own)


def solution(mesh):
    block = P("member", "horiz", "vert", None)
    return jax.shard_map(
        local,
        mesh=mesh,
        in_specs=(block, block, P("vert"), P(), P(), P(), P(), P(), P("member")),
        out_specs=(block, block),
        check_vma=False,
    )
```

```python
import functools

import jax
import jax.numpy as jnp
from jax import lax
from jax.experimental import pallas as pl
from jax.experimental.pallas import tpu as pltpu
from jax.sharding import PartitionSpec as P

courant = 0.2
wavelet = (1.0, -0.5)
pair_table = ((0, 3, 4), (3, 1, 5), (4, 5, 2))
front = (0, 3, 4)
top = (3, 1, 5)
PAD = 8
ANY = pl.BlockSpec(memory_space=pl.ANY)
HBM = pl.BlockSpec(memory_space=pltpu.HBM)
VMEM = pl.BlockSpec(memory_space=pltpu.VMEM)
SMEM = pl.BlockSpec(memory_space=pltpu.SMEM)


def swap_pairs(sizes, along, odd):
    members, rows, cols = sizes
    out = []
    for a in range(members):
        for i in range(rows):
            for j in range(cols):
                here = [a, i, j]
                there = [a, i, j]
                if not odd:
                    there[along] ^= 1
                elif 0 < here[along] < sizes[along] - 1:
                    there[along] += 1 if here[along] % 2 else -1
                else:
                    there[1 if along == 2 else 2 if members % 2 else 0] ^= 1
                out.append(tuple((p[0] * rows + p[1]) * cols + p[2] for p in (here, there)))
    return out


def swap(block, along, odd):
    axes = ("member", "horiz", "vert")
    return lax.ppermute(block, axes, swap_pairs([lax.axis_size(a) for a in axes], along, odd))


def lane_of(shape):
    return lax.broadcasted_iota(jnp.int32, shape, len(shape) - 1)


def back_lane(a):
    moved = pltpu.roll(a, 1, 1)
    return a - jnp.where(lane_of(a.shape) == 0, 0.0, moved)


def fore_lane(a):
    last = a.shape[-1] - 1
    moved = pltpu.roll(a, last, 1)
    return jnp.where(lane_of(a.shape) == last, 0.0, moved) - a


def velocity_tile(s_at, v_at, rb, dq):
    out = []
    for k in range(3):
        a, b, c = pair_table[k]
        total = (s_at(a, 0, 0) - s_at(a, -1, 0)) + (s_at(b, 0, 0) - s_at(b, 0, -1))
        total = total + back_lane(s_at(c, 0, 0))
        out.append(dq * v_at(k) + rb * total)
    return out


def strain(v_at):
    grads = []
    for i in range(3):
        here = v_at(i, 0, 0)
        grads.append([v_at(i, 1, 0) - here, v_at(i, 0, 1) - here, fore_lane(here)])
    return grads


def stress_terms(g, rl, rm, wanted=range(6)):
    out = {}
    if any(c < 3 for c in wanted):
        spread = rl * (g[0][0] + g[1][1] + g[2][2])
    for c in wanted:
        if c < 3:
            out[c] = spread + 2.0 * rm * g[c][c]
        else:
            i, j = ((0, 1), (0, 2), (1, 2))[c - 3]
            out[c] = rm * (g[i][j] + g[j][i])
    return out


def memo(fn):
    seen = {}

    def call(*key):
        if key not in seen:
            seen[key] = fn(*key)
        return seen[key]

    return call


MSG = 200


def level_scalars(index_ref, table_ref, z):
    kind = index_ref[z]
    return (
        courant * table_ref[0, kind],
        1.0 - courant * table_ref[3, kind],
        courant * table_ref[1, kind],
        courant * table_ref[2, kind],
    )


def edge_kernel(
    n, m, y, v_ref, s_ref, index, table, out_a, out_b, coef, low, high, index_ref, table_ref, sems
):
    vert = lax.axis_index("vert")
    odd = vert % 2 == 1
    copies = []
    for at, (buf, start) in enumerate(((low, 0), (high, m - 8))):
        copies.append(
            pltpu.make_async_copy(s_ref.at[:, :, pl.ds(start, 8), :], buf.at[pl.ds(0, 6), pl.ds(1, n)], sems.at[2 * at])
        )
        copies.append(
            pltpu.make_async_copy(
                v_ref.at[:, :, pl.ds(start, 8), :], buf.at[pl.ds(6, 3), pl.ds(1, n)], sems.at[2 * at + 1]
            )
        )
    scalars = [
        pltpu.make_async_copy(src, dst, sems.at[4 + i])
        for i, (src, dst) in enumerate(((index, index_ref), (table, table_ref)))
    ]
    for copy in scalars + copies:
        copy.start()
    for buf in (low, high):
        for f in front:
            buf[f, 0] = jnp.zeros((8, y), jnp.float32)
    for copy in scalars:
        copy.wait()
    at_first = level_scalars(index_ref, table_ref, 0)
    at_second = level_scalars(index_ref, table_ref, 1)
    at_last = level_scalars(index_ref, table_ref, m - 1)

    def level(z, carry):
        for c, value in enumerate(level_scalars(index_ref, table_ref, z)):
            coef[c, pl.ds(PAD + z, 1), :] = jnp.full((1, y), value, jnp.float32)
        return carry

    lax.fori_loop(0, m, level, 0, unroll=8)
    for copy in copies:
        copy.wait()
    low2 = low.reshape(9 * (n + 2) * 8, y)
    high2 = high.reshape(9 * (n + 2) * 8, y)

    def row(buf, f, z, dx=0):
        return buf[pl.Slice((f * (n + 2) + 1 + dx) * 8 + z, n, 8), :]

    def moved(buf, z, scal):
        return velocity_tile(
            memo(lambda f, dx, dz: row(buf, f, z + dz, dx)), lambda k: row(buf, 6 + k, z), scal[0], scal[1]
        )

    up = [row(high2, f, 7) for f in range(6)] + moved(high2, 7, at_last)
    down = [row(low2, f, 0) for f in range(9)] + moved(low2, 1, at_second)

    def put(at, rows, up_value, down_value):
        out_a[pl.ds(at, rows), :] = jnp.where(odd, down_value, up_value)
        out_b[pl.ds(at, rows), :] = jnp.where(odd, up_value, down_value)

    for f in range(12):
        put(f * n, n, up[f] if f < 9 else down[f], down[f])
    base = 12 * n
    for c in range(4):
        splat = [jnp.full((1, y), a[c], jnp.float32) for a in (at_last, at_first)]
        put(base + c, 1, *splat)
    ahead = jnp.full((1, y), at_second[0], jnp.float32)
    put(base + 4, 1, ahead, ahead)
    for c, f in enumerate(front):
        corner = low[f, n, pl.ds(1, 1), :]
        put(base + 5 + c, 1, corner, corner)


EDGE_MIB, LOAD_MIB, SMALL_MIB = 16, 16, 16
GROUP = 8


def load_kernel(n, m, y, v_ref, s_ref, coef_in, split, *refs):
    sources, (vb, sb, raw, coef), scratch = refs[:4], refs[4:8], refs[8:]
    sx, sz, sy, amp, small = scratch
    del coef_in
    fetched = fetch_sources(sources, (sx, sz, sy, amp), small)
    for f in front:
        sb[f, 0] = jnp.zeros((m + 16, y), jnp.float32)
    for k in range(3):
        vb[k, n + 1] = jnp.zeros((m + 16, y), jnp.float32)
    lowest, first = PAD - 1, PAD + m
    s_line, v_line, s2, v2 = lines(n, m, y, vb, sb)
    zero = jnp.zeros((n, y), jnp.float32)
    for f in range(6):
        s2[s_line(f, lowest), :] = zero
        s2[s_line(f, first), :] = zero
    for k in range(3):
        v2[v_line(k, first), :] = zero
    coef[3, pl.ds(lowest, 1), :] = jnp.ones((1, y), jnp.float32)
    coef[3, pl.ds(first, 1), :] = jnp.ones((1, y), jnp.float32)
    start = split[0] - lax.axis_index("vert") * m
    tiles = [PAD + 8 * t for t in range(m // 8)]
    for r, size in [(r, 8) for r in tiles] + [(lowest, 1), (first, 1)]:
        level = r - PAD + lax.broadcasted_iota(jnp.int32, (size, y), 0)
        at = pl.ds(r, size)
        coef[3, at, :] = jnp.where(level >= start, coef[3, at, :], 0.0)

    def cs(c, r):
        return coef[c, pl.ds(r, 8), :]

    def move(x, first_group=False):
        for r in tiles:
            rb, dq = cs(0, r), cs(1, r)

            def stress_of(f, p, dz):
                if p < 0 and first_group:
                    return 0.0
                if dz and r == PAD:
                    return plane_before(s_ref[f, x + p, pl.ds(0, 8), :])
                return s_ref[f, x + p, pl.ds(r - PAD + dz, 8), :]

            stress_of = memo(stress_of)
            for p in range(GROUP):
                new = velocity_tile(
                    lambda f, dx, dz: stress_of(f, p + dx, dz), lambda k: v_ref[k, x + p, pl.ds(r - PAD, 8), :], rb, dq
                )
                for k in range(3):
                    vb[k, x + p + 1, pl.ds(r, 8), :] = new[k]

    def load(g, carry):
        x = GROUP * g
        for r in tiles:
            rl, rm = cs(2, r), cs(3, r)
            speed_of = memo(lambda k, p, dz: vb[k, x + p + 1, pl.ds(r + dz, 8), :])
            for p in range(GROUP):
                terms = stress_terms(strain(lambda k, dx, dz: speed_of(k, p + dx, dz)), rl, rm)
                for c in range(6):
                    sb[c, x + p + 1, pl.ds(r, 8), :] = s_ref[c, x + p, pl.ds(r - PAD, 8), :] + terms[c]
        return carry

    move(0, True)
    lax.fori_loop(1, n // GROUP, lambda g, carry: (move(GROUP * g), carry)[1], 0)
    lax.fori_loop(0, n // GROUP, load, 0)
    for c, f in enumerate(front):
        raw[c] = s_ref[f, n - 1]
    for copy in fetched:
        copy.wait()
    x_at, z_at = lax.axis_index("horiz") * n, lax.axis_index("vert") * m

    def add(i, carry):
        x, z = sx[i] - x_at, sz[i] - z_at

        @pl.when((x >= 0) & (x < n) & (z >= -1) & (z <= m))
        def _():
            row = jnp.where(lane_of((1, y)) == sy[i], courant * wavelet[0] * amp[i], 0.0)
            at = pl.ds(PAD + z, 1)
            for c in range(3):
                sb[c, x + 1, at, :] = sb[c, x + 1, at, :] + row

        return carry

    lax.fori_loop(0, sx.shape[0], add, 0)


def lines(n, m, y, vb, sb):
    high = m + 16

    def s_line(f, r):
        return pl.Slice((f * (n + 2) + 1) * high + r, n, high)

    def v_line(k, r):
        return pl.Slice((k * (n + 2) + 1) * high + r, n, high)

    return s_line, v_line, sb.reshape(6 * (n + 2) * high, y), vb.reshape(3 * (n + 2) * high, y)


def plane_before(a):
    rows = lax.broadcasted_iota(jnp.int32, a.shape, 0)
    return jnp.where(rows == 0, 0.0, pltpu.roll(a, 1, 0))


def plane_after(a):
    last = a.shape[0] - 1
    rows = lax.broadcasted_iota(jnp.int32, a.shape, 0)
    return jnp.where(rows == last, 0.0, pltpu.roll(a, last, 0))


def fetch_sources(refs, held, sems):
    copies = [pltpu.make_async_copy(src, dst, sems.at[i]) for i, (src, dst) in enumerate(zip(refs, held))]
    for copy in copies:
        copy.start()
    return copies


def plane_kernel(n, m, y, got_a, got_b, edge_a, edge_b, v_in, s_in, raw, coef_in, out_a, out_b, vb, sb, coef, below, above):
    del v_in, s_in, coef_in
    horiz, vert = lax.axis_index("horiz"), lax.axis_index("vert")
    odd = vert % 2 == 1
    has_below = jnp.where(vert > 0, 1.0, 0.0)
    has_above = jnp.where(vert < lax.axis_size("vert") - 1, 1.0, 0.0)
    for t in range(MSG // 8):
        at = pl.ds(8 * t, 8)
        a, b = got_a[at, :], got_b[at, :]
        below[at, :] = has_below * jnp.where(odd, a, b)
        above[at, :] = has_above * jnp.where(odd, b, a)
    lowest, first, second = PAD - 1, PAD + m, PAD + m + 1
    base = 12 * n
    for c in range(4):
        for r, side in ((lowest, below), (first, above)):
            value = side[pl.ds(base + c, 1), :]
            coef[c, pl.ds(r, 1), :] = value * coef[c, pl.ds(r, 1), :] if c == 3 else value
    coef[0, pl.ds(second, 1), :] = above[pl.ds(base + 4, 1), :]

    def cs(c, r, size):
        return coef[c, pl.ds(r, size), :]

    s_line, v_line, s2, v2 = lines(n, m, y, vb, sb)
    low = [below[pl.ds(f * n, n), :] for f in range(9)]
    high = [above[pl.ds(f * n, n), :] for f in range(12)]
    own = [None] * 6
    for f in top:
        at = pl.ds(f * n, n)
        own[f] = jnp.where(odd, edge_b[at, :], edge_a[at, :])

    def beyond(f, dx, dz):
        if dz:
            return own[f]
        return plane_before(high[f]) if dx else high[f]

    v_high = velocity_tile(memo(beyond), lambda k: high[6 + k], cs(0, first, 1), cs(1, first, 1))
    change = [-cs(0, PAD, 1) * low[top[k]] for k in range(3)]
    v_low = [v2[v_line(k, PAD), :] + change[k] for k in range(3)]
    for k in range(3):
        v2[v_line(k, first), :] = v_high[k]
        v2[v_line(k, PAD), :] = v_low[k]

    def add_terms(r, grads, wanted, start=None):
        terms = stress_terms(grads, cs(2, r, 1), cs(3, r, 1), wanted)
        for c in wanted:
            line = s_line(c, r)
            old = s2[line, :]
            s2[line, :] = old + terms[c] if start is None else old + (start[c] + terms[c])

    def across(v):
        return [plane_after(v) - v, None, fore_lane(v)]

    def grads_of(values, next_values):
        out = []
        for v, after in zip(values, next_values):
            grad = across(v)
            grad[1] = -v if after is None else after - v
            out.append(grad)
        return out

    add_terms(lowest, grads_of(low[6:9], v_low), top, low)
    add_terms(PAD, grads_of(change, [None] * 3), range(6))
    add_terms(first, grads_of(v_high, high[9:12]), range(6), high)
    rl, rm = cs(2, first - 1, 1), cs(3, first - 1, 1)
    spread = rl * v_high[1]
    for c, term in ((0, spread), (1, spread + 2.0 * rm * v_high[1]), (2, spread), (3, rm * v_high[0]), (5, rm * v_high[2])):
        line = s_line(c, first - 1)
        s2[line, :] = s2[line, :] + term

    even = horiz % 2 == 0
    tiles = [(PAD + 8 * t, 8) for t in range(m // 8)]
    tail = 6 * m

    def put(at, size, to_right, to_left):
        out_a[pl.ds(at, size), :] = jnp.where(even, to_right, to_left)
        out_b[pl.ds(at, size), :] = jnp.where(even, to_left, to_right)

    for r, size in tiles:
        new = velocity_tile(
            memo(lambda f, dx, dz: 0.0 if dx else sb[f, 1, pl.ds(r + dz, size), :]),
            lambda k: vb[k, 1, pl.ds(r, size), :],
            cs(0, r, size),
            cs(1, r, size),
        )
        for c, f in enumerate(front):
            put(c * m + r - PAD, size, raw[c, pl.ds(r - PAD, size), :], vb[c, 1, pl.ds(r, size), :])
            put((3 + c) * m + r - PAD, size, sb[f, n, pl.ds(r, size), :], new[c])
    for c, f in enumerate(front):
        last = f * n + n - 1
        before_low, before_first = below[pl.ds(last, 1), :], above[pl.ds(last, 1), :]
        put(tail + c, 1, before_low, below[pl.ds((6 + c) * n, 1), :])
        put(tail + 3 + c, 1, before_first, vb[c, 1, pl.ds(first, 1), :])
        before_second, after_first = above[pl.ds(base + 5 + c, 1), :], sb[f, n, pl.ds(first, 1), :]
        put(tail + 6 + c, 1, before_second, before_second)
        put(tail + 9 + c, 1, after_first, after_first)


def rest_kernel(n, m, y, v_in, s_in, coef, *refs):
    sources, (vb, sb, out_v, out_s), scratch = refs[:4], refs[4:8], refs[8:]
    sx, sz, sy, amp, near_x, near_z, near_y, near_amp, small, sems = scratch
    del v_in, s_in
    horiz, vert = lax.axis_index("horiz"), lax.axis_index("vert")
    fetched = fetch_sources(sources, (sx, sz, sy, amp), small)
    body = pl.ds(PAD, m)
    first = PAD + m
    tiles = [(PAD + 8 * t, 8) for t in range(m // 8)]

    def cs(c, r, size):
        return coef[c, pl.ds(r, size), :]

    s_line, v_line, s2, v2 = lines(n, m, y, vb, sb)

    def beyond(f, dx, dz):
        here = s2[s_line(f, first + dz), :]
        return plane_before(here) if dx else here

    new = velocity_tile(memo(beyond), lambda k: v2[v_line(k, first), :], cs(0, first, 1), cs(1, first, 1))
    for k in range(3):
        v2[v_line(k, first), :] = new[k]

    def move(x, planes):
        for r, size in tiles:
            rb, dq = cs(0, r, size), cs(1, r, size)
            stress_of = memo(lambda f, p, dz: sb[f, x + p + 1, pl.ds(r + dz, size), :])
            for p in range(planes):
                new = velocity_tile(
                    lambda f, dx, dz: stress_of(f, p + dx, dz), lambda k: vb[k, x + p + 1, pl.ds(r, size), :], rb, dq
                )
                for k in range(3):
                    vb[k, x + p + 1, pl.ds(r, size), :] = new[k]

    def load(x, planes):
        for r, size in tiles:
            rl, rm = cs(2, r, size), cs(3, r, size)
            speed_of = memo(lambda k, p, dz: vb[k, x + p + 1, pl.ds(r + dz, size), :])
            for p in range(planes):
                terms = stress_terms(strain(lambda k, dx, dz: speed_of(k, p + dx, dz)), rl, rm)
                for c in range(6):
                    sb[c, x + p + 1, pl.ds(r, size), :] = sb[c, x + p + 1, pl.ds(r, size), :] + terms[c]

    for copy in fetched:
        copy.wait()
    found = jnp.int32(0)
    for i in range(sx.shape[0]):
        x, z = sx[i] - horiz * n, sz[i] - vert * m
        near_x[found], near_z[found], near_y[found], near_amp[found] = x, z, sy[i], amp[i]
        found = found + ((x >= 0) & (x < n) & (z >= 0) & (z < m)).astype(jnp.int32)

    def add_near(x_low, x_high):
        def add(j, carry):
            x, z = near_x[j], near_z[j]

            @pl.when((x >= x_low) & (x < x_high))
            def _():
                row = jnp.where(lane_of((1, y)) == near_y[j], courant * wavelet[1] * near_amp[j], 0.0)
                at = pl.ds(PAD + z, 1)
                for c in range(3):
                    sb[c, x + 1, at, :] = sb[c, x + 1, at, :] + row

            return carry

        lax.fori_loop(0, found, add, 0)

    def v_off(x):
        return pltpu.make_async_copy(vb.at[:, x + 1, body], out_v.at[:, x], sems.at[0, x])

    def s_off(x):
        return pltpu.make_async_copy(sb.at[:, x + 1, body], out_s.at[:, x], sems.at[1, x])

    def send(off, x, end):
        @pl.when((x >= 2) & (x < end))
        def _():
            off(x).start()

    def advance(x, planes):
        move(x, planes)
        for p in range(planes):
            send(v_off, x + p, n - 1)
        load(x - 1, planes)
        add_near(x - 1, x + planes - 1)
        for p in range(-1, planes - 1):
            send(s_off, x + p, n - 2)

    lax.fori_loop(0, n // GROUP - 1, lambda g, carry: (advance(GROUP * g, GROUP), carry)[1], 0)
    for x, planes in ((n - GROUP, GROUP - 4), (n - 4, 2), (n - 2, 2)):
        advance(x, planes)
    load(n - 1, 1)
    add_near(n - 1, n)

    def finish(x, carry):
        v_off(x).wait()
        s_off(x).wait()
        return carry

    lax.fori_loop(2, n - 2, finish, 0)
    v_off(n - 2).wait()


def join_kernel(n, m, y, next_b, next_a, own_a, own_b, coef, vb, sb, v_in, s_in, v_out, s_out, *scratch):
    wa, da, ds, dv, dw, qb, db, es, ev, vn, v0, v1, s0, s1, sems = scratch
    del v_in, s_in
    horiz = lax.axis_index("horiz")
    even = horiz % 2 == 0
    has_left = jnp.where(horiz > 0, 1.0, 0.0)
    has_right = jnp.where(horiz < lax.axis_size("horiz") - 1, 1.0, 0.0)
    lowest, first, second = PAD - 1, PAD + m, PAD + m + 1
    tail = 6 * m
    tiles = [(PAD + 8 * t, 8) for t in range(m // 8)]

    def cs(c, r, size):
        return coef[c, pl.ds(r, size), :]

    pick = {"right": (next_a, next_b), "left": (next_b, next_a), "own right": (own_a, own_b), "own left": (own_b, own_a)}

    def rows_of(which, at, size):
        a, b = pick[which]
        return jnp.where(even, a[pl.ds(at, size), :], b[pl.ds(at, size), :])

    def msg(which, c, r, size):
        return rows_of(which, c * m + r - PAD, size)

    def end(which, at):
        return rows_of(which, tail + at, 1)

    for k in range(3):
        rows = [(r, size, msg("left", k, r, size)) for r, size in tiles]
        rows += [(r, 1, end("left", at + k)) for r, at in ((lowest, 0), (first, 3), (second, 6))]
        for r, size, value in rows:
            da[k, pl.ds(r, size), :] = -(has_left * cs(0, r, size)) * value
        rows = [(r, size, msg("left", 3 + k, r, size), msg("own left", k, r, size)) for r, size in tiles]
        rows += [(first, 1, end("left", 9 + k), end("own left", 3 + k))]
        for r, size, value, own in rows:
            gain = cs(3, r, size) if k else cs(2, r, size) + 2.0 * cs(3, r, size)
            wa[k, pl.ds(r, size), :] = has_left * (value + gain * (own + da[k, pl.ds(r, size), :]))
        rows = [(r, size, msg("own right", k, r, size), msg("right", k, r, size)) for r, size in tiles]
        rows += [(r, 1, end("own right", at + k), end("right", at + k)) for r, at in ((lowest, 0), (first, 3))]
        for r, size, value, other in rows:
            change = -(has_right * cs(0, r, size)) * value
            db[k, pl.ds(r, size), :] = change
            qb[k, pl.ds(r, size), :] = has_right * other + change

    def strain_of(buf, r, size, ahead=None):
        grads = []
        for i in range(3):
            here = buf[i, pl.ds(r, size), :]
            beyond = -here if ahead is None else ahead[i, pl.ds(r, size), :] - here
            grads.append([beyond, buf[i, pl.ds(r + 1, size), :] - here, fore_lane(here)])
        return grads

    for out, src, ends in ((ds, da, (lowest, first)), (es, db, (lowest,))):
        parts = [(r, size, range(6)) for r, size in tiles]
        parts += [(r, 1, top if r == lowest else range(6)) for r in ends]
        for r, size, wanted in parts:
            terms = stress_terms(strain_of(src, r, size), cs(2, r, size), cs(3, r, size), wanted)
            for c in wanted:
                out[c, pl.ds(r, size), :] = terms[c]

    for r, size in tiles + [(first, 1)]:
        rb, dq = cs(0, r, size), cs(1, r, size)
        for k in range(3):
            a, b, c = pair_table[k]
            here = ds[a, pl.ds(r, size), :]
            total = here - wa[k, pl.ds(r, size), :]
            total = total + (ds[b, pl.ds(r, size), :] - ds[b, pl.ds(r - 1, size), :])
            total = total + back_lane(ds[c, pl.ds(r, size), :])
            dv[k, pl.ds(r, size), :] = dq * da[k, pl.ds(r, size), :] + rb * total
            dw[k, pl.ds(r, size), :] = -rb * here

    def last_stress(c, r, size):
        q = qb[0 if c < 3 else c - 2, pl.ds(r, size), :]
        if c == 0:
            return (cs(2, r, size) + 2.0 * cs(3, r, size)) * q
        return (cs(2, r, size) if c < 3 else cs(3, r, size)) * q

    for r, size in tiles + [(first, 1)]:
        rb, dq = cs(0, r, size), cs(1, r, size)
        full = [last_stress(c, r, size) for c in range(5)]
        totals = [
            full[0] + (full[3] - last_stress(3, r - 1, size)) + back_lane(full[4]),
            full[3] + (full[1] - last_stress(1, r - 1, size)),
            full[4] + back_lane(full[2]),
        ]
        for k in range(3):
            ev[k, pl.ds(r, size), :] = rb * totals[k]
        if r == first:
            continue
        for k in range(3):
            a, b, c = pair_table[k]
            total = es[a, pl.ds(r, size), :] - (msg("own right", 3 + k, r, size) + full[a])
            total = total + (es[b, pl.ds(r, size), :] - es[b, pl.ds(r - 1, size), :])
            total = total + back_lane(es[c, pl.ds(r, size), :])
            change = dq * db[k, pl.ds(r, size), :] + rb * total
            vn[k, pl.ds(r, size), :] = has_right * (msg("right", 3 + k, r, size) + change)

    def put(buf, dst, x, i):
        copy = pltpu.make_async_copy(buf, dst.at[:, x], sems.at[i])
        copy.start()
        return copy

    copies = []
    for buf, x, change in ((v0.at[:, 0], 0, dv), (v0.at[:, 1], 1, dw), (v1.at[:, 0], n - 1, ev)):
        for r, size in tiles:
            out, at = pl.ds(r - PAD, size), pl.ds(r, size)
            for k in range(3):
                buf[k, out, :] = vb[k, x + 1, at, :] + change[k, at, :]
        copies.append(put(buf, v_out, x, len(copies)))
    for buf, x, src, ahead, more in (
        (s0.at[:, 0], 0, dv, dw, lambda c, r: ds[c, pl.ds(r, 8), :]),
        (s0.at[:, 1], 1, dw, None, None),
        (s1.at[:, 0], n - 1, ev, vn, lambda c, r: None if c == 5 else last_stress(c, r, 8)),
    ):
        for r, size in tiles:
            out, at = pl.ds(r - PAD, size), pl.ds(r, size)
            terms = stress_terms(strain_of(src, r, size, ahead), cs(2, r, size), cs(3, r, size))
            for c in range(6):
                extra = None if more is None else more(c, r)
                term = terms[c] if extra is None else terms[c] + extra
                buf[c, out, :] = sb[c, x + 1, at, :] + term
        copies.append(put(buf, s_out, x, len(copies)))
    for r, size in tiles:
        out, at = pl.ds(r - PAD, size), pl.ds(r, size)
        rl, rm = cs(2, r, size), cs(3, r, size)
        e = [ev[k, at, :] for k in range(3)]
        spread = rl * e[0]
        for c, term in enumerate((spread + 2.0 * rm * e[0], spread, spread, rm * e[1], rm * e[2], None)):
            old = sb[c, n - 1, at, :]
            s1[c, 1, out, :] = old if term is None else old + term
    copies.append(put(s1.at[:, 1], s_out, n - 2, len(copies)))
    for copy in copies:
        copy.wait()


def local(velocity, stress, index, table, split, source_x, source_z, source_y, amplitude):
    _, n, m, y = velocity.shape
    f32, i32 = jnp.float32, jnp.int32
    high = m + 16
    dma = pltpu.SemaphoreType.DMA
    sources = (source_x, source_z, source_y, amplitude)
    held = [pltpu.SMEM(a.shape, a.dtype) for a in sources]
    near = [pltpu.SMEM((a.shape[0] + 1,), a.dtype) for a in sources]
    table = table.T
    materials = [pltpu.SMEM((m,), i32), pltpu.SMEM(table.shape, f32)]

    def shape(*dims):
        return jax.ShapeDtypeStruct(dims, f32)

    def kept(*dims):
        return pltpu.VMEM(dims, f32)

    def outside(*dims):
        return pltpu.HBM(dims, f32)

    def room(mib):
        return pltpu.CompilerParams(vmem_limit_bytes=mib * 1024 * 1024)

    def cost(flops, moved):
        return pl.CostEstimate(flops=flops, bytes_accessed=moved, transcendentals=0)

    padded_v, padded_s = kept(3, n + 2, high, y), kept(6, n + 2, high, y)
    edge_a, edge_b, coef = pl.pallas_call(
        functools.partial(edge_kernel, n, m, y),
        out_shape=[kept(MSG, y)] * 2 + [kept(4, high, y)],
        in_specs=[HBM] * 4,
        out_specs=[VMEM] * 3,
        scratch_shapes=[pltpu.VMEM((9, n + 2, 8, y), f32)] * 2 + materials + [dma((6,))],
        compiler_params=room(EDGE_MIB),
        name="edge_levels",
    )(*[pltpu.with_memory_space_constraint(a, pltpu.HBM) for a in (velocity, stress, index, table)])
    got_a, got_b = swap(edge_a, 2, False), swap(edge_b, 2, True)
    split, edge_a = lax.optimization_barrier((split, edge_a))
    vb, sb, raw, coef = pl.pallas_call(
        functools.partial(load_kernel, n, m, y),
        out_shape=[padded_v, padded_s, kept(3, m, y), kept(4, high, y)],
        in_specs=[VMEM, VMEM, VMEM, SMEM] + [ANY] * 4,
        out_specs=[VMEM] * 4,
        input_output_aliases={2: 3},
        scratch_shapes=[*held, dma((4,))],
        compiler_params=room(LOAD_MIB),
        cost_estimate=cost(60 * n * m * y, 4 * 9 * n * m * y),
        name="load_block",
    )(*[pltpu.with_memory_space_constraint(a, pltpu.VMEM) for a in (velocity, stress)], coef, split, *sources)
    plane_a, plane_b, vb, sb, coef = pl.pallas_call(
        functools.partial(plane_kernel, n, m, y),
        out_shape=[kept(6 * m + 16, y)] * 2 + [padded_v, padded_s, kept(4, high, y)],
        in_specs=[VMEM] * 8,
        out_specs=[VMEM] * 5,
        input_output_aliases={4: 2, 5: 3, 7: 4},
        scratch_shapes=[pltpu.VMEM((MSG, y), f32)] * 2,
        compiler_params=room(SMALL_MIB),
        name="edge_planes",
    )(got_a, got_b, edge_a, edge_b, vb, sb, raw, coef)
    next_b = swap(plane_b, 1, True)
    next_a = swap(plane_a, 1, False)
    vb, sb, v_own, s_own = pl.pallas_call(
        functools.partial(rest_kernel, n, m, y),
        out_shape=[padded_v, padded_s, outside(*velocity.shape), outside(*stress.shape)],
        in_specs=[VMEM] * 3 + [ANY] * 4,
        out_specs=[VMEM, VMEM, HBM, HBM],
        input_output_aliases={0: 0, 1: 1},
        scratch_shapes=[*held, *near, dma((4,)), dma((2, n))],
        compiler_params=room(SMALL_MIB),
        cost_estimate=cost(60 * n * m * y, 4 * 9 * n * m * y),
        name="both_steps",
    )(vb, sb, coef, *sources)
    plane = pltpu.VMEM((3, high, y), f32)
    plane6 = pltpu.VMEM((6, high, y), f32)
    return pl.pallas_call(
        functools.partial(join_kernel, n, m, y),
        out_shape=[outside(*velocity.shape), outside(*stress.shape)],
        in_specs=[VMEM] * 7 + [HBM] * 2,
        out_specs=[HBM, HBM],
        input_output_aliases={7: 0, 8: 1},
        scratch_shapes=[plane, plane, plane6, plane, plane, plane, plane, plane6, plane, plane]
        + [pltpu.VMEM((3, 2, m, y), f32), pltpu.VMEM((3, 1, m, y), f32)]
        + [pltpu.VMEM((6, 2, m, y), f32)] * 2
        + [dma((7,))],
        compiler_params=room(SMALL_MIB),
        name="join_neighbours",
    )(next_b, next_a, plane_a, plane_b, coef, vb, sb, v_own, s_own)


def solution(mesh):
    block = P("member", "horiz", "vert", None)
    return jax.shard_map(
        local,
        mesh=mesh,
        in_specs=(block, block, P("vert"), P(), P(), P(), P(), P(), P("member")),
        out_specs=(block, block),
        check_vma=False,
    )
```

```python
import functools

import jax
import jax.numpy as jnp
from jax import lax
from jax.experimental import pallas as pl
from jax.experimental.pallas import tpu as pltpu
from jax.sharding import PartitionSpec as P

courant = 0.2
wavelet = (1.0, -0.5)
pair_table = ((0, 3, 4), (3, 1, 5), (4, 5, 2))
front = (0, 3, 4)
top = (3, 1, 5)
PAD = 8
ANY = pl.BlockSpec(memory_space=pl.ANY)
HBM = pl.BlockSpec(memory_space=pltpu.HBM)
VMEM = pl.BlockSpec(memory_space=pltpu.VMEM)
SMEM = pl.BlockSpec(memory_space=pltpu.SMEM)


def swap_pairs(sizes, along, odd):
    members, rows, cols = sizes
    out = []
    for a in range(members):
        for i in range(rows):
            for j in range(cols):
                here = [a, i, j]
                there = [a, i, j]
                if not odd:
                    there[along] ^= 1
                elif 0 < here[along] < sizes[along] - 1:
                    there[along] += 1 if here[along] % 2 else -1
                else:
                    there[1 if along == 2 else 2 if members % 2 else 0] ^= 1
                out.append(tuple((p[0] * rows + p[1]) * cols + p[2] for p in (here, there)))
    return out


def swap(block, along, odd):
    axes = ("member", "horiz", "vert")
    return lax.ppermute(block, axes, swap_pairs([lax.axis_size(a) for a in axes], along, odd))


def lane_of(shape):
    return lax.broadcasted_iota(jnp.int32, shape, len(shape) - 1)


def back_lane(a):
    moved = pltpu.roll(a, 1, 1)
    return a - jnp.where(lane_of(a.shape) == 0, 0.0, moved)


def fore_lane(a):
    last = a.shape[-1] - 1
    moved = pltpu.roll(a, last, 1)
    return jnp.where(lane_of(a.shape) == last, 0.0, moved) - a


def velocity_tile(s_at, v_at, rb, dq):
    out = []
    for k in range(3):
        a, b, c = pair_table[k]
        total = (s_at(a, 0, 0) - s_at(a, -1, 0)) + (s_at(b, 0, 0) - s_at(b, 0, -1))
        total = total + back_lane(s_at(c, 0, 0))
        out.append(dq * v_at(k) + rb * total)
    return out


def strain(v_at):
    grads = []
    for i in range(3):
        here = v_at(i, 0, 0)
        grads.append([v_at(i, 1, 0) - here, v_at(i, 0, 1) - here, fore_lane(here)])
    return grads


def stress_terms(g, rl, rm, wanted=range(6)):
    out = {}
    if any(c < 3 for c in wanted):
        spread = rl * (g[0][0] + g[1][1] + g[2][2])
    for c in wanted:
        if c < 3:
            out[c] = spread + 2.0 * rm * g[c][c]
        else:
            i, j = ((0, 1), (0, 2), (1, 2))[c - 3]
            out[c] = rm * (g[i][j] + g[j][i])
    return out


def memo(fn):
    seen = {}

    def call(*key):
        if key not in seen:
            seen[key] = fn(*key)
        return seen[key]

    return call


MSG = 200


def level_scalars(index_ref, table_ref, z):
    kind = index_ref[z]
    return (
        courant * table_ref[0, kind],
        1.0 - courant * table_ref[3, kind],
        courant * table_ref[1, kind],
        courant * table_ref[2, kind],
    )


def edge_kernel(
    n, m, y, v_ref, s_ref, index, table, out_a, out_b, coef, low, high, index_ref, table_ref, sems
):
    vert = lax.axis_index("vert")
    odd = vert % 2 == 1
    copies = []
    for at, (buf, start) in enumerate(((low, 0), (high, m - 8))):
        copies.append(
            pltpu.make_async_copy(s_ref.at[:, :, pl.ds(start, 8), :], buf.at[pl.ds(0, 6), pl.ds(1, n)], sems.at[2 * at])
        )
        copies.append(
            pltpu.make_async_copy(
                v_ref.at[:, :, pl.ds(start, 8), :], buf.at[pl.ds(6, 3), pl.ds(1, n)], sems.at[2 * at + 1]
            )
        )
    scalars = [
        pltpu.make_async_copy(src, dst, sems.at[4 + i])
        for i, (src, dst) in enumerate(((index, index_ref), (table, table_ref)))
    ]
    for copy in scalars + copies:
        copy.start()
    for buf in (low, high):
        for f in front:
            buf[f, 0] = jnp.zeros((8, y), jnp.float32)
    for copy in scalars:
        copy.wait()
    at_first = level_scalars(index_ref, table_ref, 0)
    at_second = level_scalars(index_ref, table_ref, 1)
    at_last = level_scalars(index_ref, table_ref, m - 1)

    def level(z, carry):
        for c, value in enumerate(level_scalars(index_ref, table_ref, z)):
            coef[c, pl.ds(PAD + z, 1), :] = jnp.full((1, y), value, jnp.float32)
        return carry

    lax.fori_loop(0, m, level, 0, unroll=8)
    for copy in copies:
        copy.wait()
    low2 = low.reshape(9 * (n + 2) * 8, y)
    high2 = high.reshape(9 * (n + 2) * 8, y)

    def row(buf, f, z, dx=0):
        return buf[pl.Slice((f * (n + 2) + 1 + dx) * 8 + z, n, 8), :]

    def moved(buf, z, scal):
        return velocity_tile(
            memo(lambda f, dx, dz: row(buf, f, z + dz, dx)), lambda k: row(buf, 6 + k, z), scal[0], scal[1]
        )

    up = [row(high2, f, 7) for f in range(6)] + moved(high2, 7, at_last)
    down = [row(low2, f, 0) for f in range(9)] + moved(low2, 1, at_second)

    def put(at, rows, up_value, down_value):
        out_a[pl.ds(at, rows), :] = jnp.where(odd, down_value, up_value)
        out_b[pl.ds(at, rows), :] = jnp.where(odd, up_value, down_value)

    for f in range(12):
        put(f * n, n, up[f] if f < 9 else down[f], down[f])
    base = 12 * n
    for c in range(4):
        splat = [jnp.full((1, y), a[c], jnp.float32) for a in (at_last, at_first)]
        put(base + c, 1, *splat)
    ahead = jnp.full((1, y), at_second[0], jnp.float32)
    put(base + 4, 1, ahead, ahead)
    for c, f in enumerate(front):
        corner = low[f, n, pl.ds(1, 1), :]
        put(base + 5 + c, 1, corner, corner)


EDGE_MIB, LOAD_MIB, SMALL_MIB = 16, 16, 16
GROUP = 8


def load_kernel(n, m, y, v_ref, s_ref, coef_in, split, *refs):
    sources, (vb, sb, raw, coef), scratch = refs[:4], refs[4:8], refs[8:]
    sx, sz, sy, amp, near_x, near_z, near_y, near_amp, small = scratch
    del coef_in
    fetched = fetch_sources(sources, (sx, sz, sy, amp), small)
    for f in front:
        sb[f, 0] = jnp.zeros((m + 16, y), jnp.float32)
    for k in range(3):
        vb[k, n + 1] = jnp.zeros((m + 16, y), jnp.float32)
    lowest, first = PAD - 1, PAD + m
    s_line, v_line, s2, v2 = lines(n, m, y, vb, sb)
    zero = jnp.zeros((n, y), jnp.float32)
    for f in range(6):
        s2[s_line(f, lowest), :] = zero
        s2[s_line(f, first), :] = zero
    for k in range(3):
        v2[v_line(k, first), :] = zero
    coef[3, pl.ds(lowest, 1), :] = jnp.ones((1, y), jnp.float32)
    coef[3, pl.ds(first, 1), :] = jnp.ones((1, y), jnp.float32)
    start = split[0] - lax.axis_index("vert") * m
    tiles = [PAD + 8 * t for t in range(m // 8)]
    for r, size in [(r, 8) for r in tiles] + [(lowest, 1), (first, 1)]:
        level = r - PAD + lax.broadcasted_iota(jnp.int32, (size, y), 0)
        at = pl.ds(r, size)
        coef[3, at, :] = jnp.where(level >= start, coef[3, at, :], 0.0)

    def cs(c, r):
        return coef[c, pl.ds(r, 8), :]

    def move(x, first_group=False):
        for r in tiles:
            rb, dq = cs(0, r), cs(1, r)

            def stress_of(f, p, dz):
                if p < 0 and first_group:
                    return 0.0
                if dz and r == PAD:
                    return plane_before(s_ref[f, x + p, pl.ds(0, 8), :])
                return s_ref[f, x + p, pl.ds(r - PAD + dz, 8), :]

            stress_of = memo(stress_of)
            for p in range(GROUP):
                new = velocity_tile(
                    lambda f, dx, dz: stress_of(f, p + dx, dz), lambda k: v_ref[k, x + p, pl.ds(r - PAD, 8), :], rb, dq
                )
                for k in range(3):
                    vb[k, x + p + 1, pl.ds(r, 8), :] = new[k]

    def load(g, carry):
        x = GROUP * g
        for r in tiles:
            rl, rm = cs(2, r), cs(3, r)
            speed_of = memo(lambda k, p, dz: vb[k, x + p + 1, pl.ds(r + dz, 8), :])
            for p in range(GROUP):
                terms = stress_terms(strain(lambda k, dx, dz: speed_of(k, p + dx, dz)), rl, rm)
                for c in range(6):
                    sb[c, x + p + 1, pl.ds(r, 8), :] = s_ref[c, x + p, pl.ds(r - PAD, 8), :] + terms[c]
        return carry

    move(0, True)
    lax.fori_loop(1, n // GROUP, lambda g, carry: (move(GROUP * g), carry)[1], 0)
    lax.fori_loop(0, n // GROUP, load, 0)
    for c, f in enumerate(front):
        raw[c] = s_ref[f, n - 1]
    for copy in fetched:
        copy.wait()
    x_at, z_at = lax.axis_index("horiz") * n, lax.axis_index("vert") * m
    found = jnp.int32(0)
    for i in range(sx.shape[0]):
        x, z = sx[i] - x_at, sz[i] - z_at
        near_x[found], near_z[found], near_y[found], near_amp[found] = x, z, sy[i], amp[i]
        found = found + ((x >= 0) & (x < n) & (z >= -1) & (z <= m)).astype(jnp.int32)

    def add(j, carry):
        x, at = near_x[j], pl.ds(PAD + near_z[j], 1)
        row = jnp.where(lane_of((1, y)) == near_y[j], courant * wavelet[0] * near_amp[j], 0.0)
        for c in range(3):
            sb[c, x + 1, at, :] = sb[c, x + 1, at, :] + row
        return carry

    lax.fori_loop(0, found, add, 0)


def lines(n, m, y, vb, sb):
    high = m + 16

    def s_line(f, r):
        return pl.Slice((f * (n + 2) + 1) * high + r, n, high)

    def v_line(k, r):
        return pl.Slice((k * (n + 2) + 1) * high + r, n, high)

    return s_line, v_line, sb.reshape(6 * (n + 2) * high, y), vb.reshape(3 * (n + 2) * high, y)


def plane_before(a):
    rows = lax.broadcasted_iota(jnp.int32, a.shape, 0)
    return jnp.where(rows == 0, 0.0, pltpu.roll(a, 1, 0))


def plane_after(a):
    last = a.shape[0] - 1
    rows = lax.broadcasted_iota(jnp.int32, a.shape, 0)
    return jnp.where(rows == last, 0.0, pltpu.roll(a, last, 0))


def fetch_sources(refs, held, sems):
    copies = [pltpu.make_async_copy(src, dst, sems.at[i]) for i, (src, dst) in enumerate(zip(refs, held))]
    for copy in copies:
        copy.start()
    return copies


def plane_kernel(n, m, y, got_a, got_b, edge_a, edge_b, v_in, s_in, raw, coef_in, out_a, out_b, vb, sb, coef, below, above):
    del v_in, s_in, coef_in
    horiz, vert = lax.axis_index("horiz"), lax.axis_index("vert")
    odd = vert % 2 == 1
    has_below = jnp.where(vert > 0, 1.0, 0.0)
    has_above = jnp.where(vert < lax.axis_size("vert") - 1, 1.0, 0.0)
    for t in range(MSG // 8):
        at = pl.ds(8 * t, 8)
        a, b = got_a[at, :], got_b[at, :]
        below[at, :] = has_below * jnp.where(odd, a, b)
        above[at, :] = has_above * jnp.where(odd, b, a)
    lowest, first, second = PAD - 1, PAD + m, PAD + m + 1
    base = 12 * n
    for c in range(4):
        for r, side in ((lowest, below), (first, above)):
            value = side[pl.ds(base + c, 1), :]
            coef[c, pl.ds(r, 1), :] = value * coef[c, pl.ds(r, 1), :] if c == 3 else value
    coef[0, pl.ds(second, 1), :] = above[pl.ds(base + 4, 1), :]

    def cs(c, r, size):
        return coef[c, pl.ds(r, size), :]

    s_line, v_line, s2, v2 = lines(n, m, y, vb, sb)
    low = [below[pl.ds(f * n, n), :] for f in range(9)]
    high = [above[pl.ds(f * n, n), :] for f in range(12)]
    own = [None] * 6
    for f in top:
        at = pl.ds(f * n, n)
        own[f] = jnp.where(odd, edge_b[at, :], edge_a[at, :])

    def beyond(f, dx, dz):
        if dz:
            return own[f]
        return plane_before(high[f]) if dx else high[f]

    v_high = velocity_tile(memo(beyond), lambda k: high[6 + k], cs(0, first, 1), cs(1, first, 1))
    change = [-cs(0, PAD, 1) * low[top[k]] for k in range(3)]
    v_low = [v2[v_line(k, PAD), :] + change[k] for k in range(3)]
    for k in range(3):
        v2[v_line(k, first), :] = v_high[k]
        v2[v_line(k, PAD), :] = v_low[k]

    def add_terms(r, grads, wanted, start=None):
        terms = stress_terms(grads, cs(2, r, 1), cs(3, r, 1), wanted)
        for c in wanted:
            line = s_line(c, r)
            old = s2[line, :]
            s2[line, :] = old + terms[c] if start is None else old + (start[c] + terms[c])

    def across(v):
        return [plane_after(v) - v, None, fore_lane(v)]

    def grads_of(values, next_values):
        out = []
        for v, after in zip(values, next_values):
            grad = across(v)
            grad[1] = -v if after is None else after - v
            out.append(grad)
        return out

    add_terms(lowest, grads_of(low[6:9], v_low), top, low)
    add_terms(PAD, grads_of(change, [None] * 3), range(6))
    add_terms(first, grads_of(v_high, high[9:12]), range(6), high)
    rl, rm = cs(2, first - 1, 1), cs(3, first - 1, 1)
    spread = rl * v_high[1]
    for c, term in ((0, spread), (1, spread + 2.0 * rm * v_high[1]), (2, spread), (3, rm * v_high[0]), (5, rm * v_high[2])):
        line = s_line(c, first - 1)
        s2[line, :] = s2[line, :] + term

    even = horiz % 2 == 0
    tiles = [(PAD + 8 * t, 8) for t in range(m // 8)]
    tail = 6 * m

    def put(at, size, to_right, to_left):
        out_a[pl.ds(at, size), :] = jnp.where(even, to_right, to_left)
        out_b[pl.ds(at, size), :] = jnp.where(even, to_left, to_right)

    for r, size in tiles:
        new = velocity_tile(
            memo(lambda f, dx, dz: 0.0 if dx else sb[f, 1, pl.ds(r + dz, size), :]),
            lambda k: vb[k, 1, pl.ds(r, size), :],
            cs(0, r, size),
            cs(1, r, size),
        )
        for c, f in enumerate(front):
            put(c * m + r - PAD, size, raw[c, pl.ds(r - PAD, size), :], vb[c, 1, pl.ds(r, size), :])
            put((3 + c) * m + r - PAD, size, sb[f, n, pl.ds(r, size), :], new[c])
    for c, f in enumerate(front):
        last = f * n + n - 1
        before_low, before_first = below[pl.ds(last, 1), :], above[pl.ds(last, 1), :]
        put(tail + c, 1, before_low, below[pl.ds((6 + c) * n, 1), :])
        put(tail + 3 + c, 1, before_first, vb[c, 1, pl.ds(first, 1), :])
        before_second, after_first = above[pl.ds(base + 5 + c, 1), :], sb[f, n, pl.ds(first, 1), :]
        put(tail + 6 + c, 1, before_second, before_second)
        put(tail + 9 + c, 1, after_first, after_first)


def rest_kernel(n, m, y, v_in, s_in, coef, *refs):
    sources, (vb, sb, out_v, out_s), scratch = refs[:4], refs[4:8], refs[8:]
    sx, sz, sy, amp, near_x, near_z, near_y, near_amp, small, sems = scratch
    del v_in, s_in
    horiz, vert = lax.axis_index("horiz"), lax.axis_index("vert")
    fetched = fetch_sources(sources, (sx, sz, sy, amp), small)
    body = pl.ds(PAD, m)
    first = PAD + m
    tiles = [(PAD + 8 * t, 8) for t in range(m // 8)]

    def cs(c, r, size):
        return coef[c, pl.ds(r, size), :]

    s_line, v_line, s2, v2 = lines(n, m, y, vb, sb)

    def beyond(f, dx, dz):
        here = s2[s_line(f, first + dz), :]
        return plane_before(here) if dx else here

    new = velocity_tile(memo(beyond), lambda k: v2[v_line(k, first), :], cs(0, first, 1), cs(1, first, 1))
    for k in range(3):
        v2[v_line(k, first), :] = new[k]

    def move(x, planes):
        for r, size in tiles:
            rb, dq = cs(0, r, size), cs(1, r, size)
            stress_of = memo(lambda f, p, dz: sb[f, x + p + 1, pl.ds(r + dz, size), :])
            for p in range(planes):
                new = velocity_tile(
                    lambda f, dx, dz: stress_of(f, p + dx, dz), lambda k: vb[k, x + p + 1, pl.ds(r, size), :], rb, dq
                )
                for k in range(3):
                    vb[k, x + p + 1, pl.ds(r, size), :] = new[k]

    def load(x, planes):
        for r, size in tiles:
            rl, rm = cs(2, r, size), cs(3, r, size)
            speed_of = memo(lambda k, p, dz: vb[k, x + p + 1, pl.ds(r + dz, size), :])
            for p in range(planes):
                terms = stress_terms(strain(lambda k, dx, dz: speed_of(k, p + dx, dz)), rl, rm)
                for c in range(6):
                    sb[c, x + p + 1, pl.ds(r, size), :] = sb[c, x + p + 1, pl.ds(r, size), :] + terms[c]

    for copy in fetched:
        copy.wait()
    found = jnp.int32(0)
    for i in range(sx.shape[0]):
        x, z = sx[i] - horiz * n, sz[i] - vert * m
        near_x[found], near_z[found], near_y[found], near_amp[found] = x, z, sy[i], amp[i]
        found = found + ((x >= 0) & (x < n) & (z >= 0) & (z < m)).astype(jnp.int32)

    def add_near(x_low, x_high):
        def add(j, carry):
            x, z = near_x[j], near_z[j]

            @pl.when((x >= x_low) & (x < x_high))
            def _():
                row = jnp.where(lane_of((1, y)) == near_y[j], courant * wavelet[1] * near_amp[j], 0.0)
                at = pl.ds(PAD + z, 1)
                for c in range(3):
                    sb[c, x + 1, at, :] = sb[c, x + 1, at, :] + row

            return carry

        lax.fori_loop(0, found, add, 0)

    def v_off(x):
        return pltpu.make_async_copy(vb.at[:, x + 1, body], out_v.at[:, x], sems.at[0, x])

    def s_off(x):
        return pltpu.make_async_copy(sb.at[:, x + 1, body], out_s.at[:, x], sems.at[1, x])

    def send(off, x, end):
        @pl.when((x >= 2) & (x < end))
        def _():
            off(x).start()

    def advance(x, planes):
        move(x, planes)
        for p in range(planes):
            send(v_off, x + p, n - 1)
        load(x - 1, planes)
        add_near(x - 1, x + planes - 1)
        for p in range(-1, planes - 1):
            send(s_off, x + p, n - 2)

    lax.fori_loop(0, n // GROUP - 1, lambda g, carry: (advance(GROUP * g, GROUP), carry)[1], 0)
    for x, planes in ((n - GROUP, GROUP - 4), (n - 4, 2), (n - 2, 2)):
        advance(x, planes)
    load(n - 1, 1)
    add_near(n - 1, n)

    def finish(x, carry):
        v_off(x).wait()
        s_off(x).wait()
        return carry

    lax.fori_loop(2, n - 2, finish, 0)
    v_off(n - 2).wait()


def join_kernel(n, m, y, next_b, next_a, own_a, own_b, coef, vb, sb, v_in, s_in, v_out, s_out, *scratch):
    wa, da, ds, dv, dw, qb, db, es, ev, vn, v0, v1, s0, s1, sems = scratch
    del v_in, s_in
    horiz = lax.axis_index("horiz")
    even = horiz % 2 == 0
    has_left = jnp.where(horiz > 0, 1.0, 0.0)
    has_right = jnp.where(horiz < lax.axis_size("horiz") - 1, 1.0, 0.0)
    lowest, first, second = PAD - 1, PAD + m, PAD + m + 1
    tail = 6 * m
    tiles = [(PAD + 8 * t, 8) for t in range(m // 8)]

    def cs(c, r, size):
        return coef[c, pl.ds(r, size), :]

    pick = {"right": (next_a, next_b), "left": (next_b, next_a), "own right": (own_a, own_b), "own left": (own_b, own_a)}

    def rows_of(which, at, size):
        a, b = pick[which]
        return jnp.where(even, a[pl.ds(at, size), :], b[pl.ds(at, size), :])

    def msg(which, c, r, size):
        return rows_of(which, c * m + r - PAD, size)

    def end(which, at):
        return rows_of(which, tail + at, 1)

    for k in range(3):
        rows = [(r, size, msg("left", k, r, size)) for r, size in tiles]
        rows += [(r, 1, end("left", at + k)) for r, at in ((lowest, 0), (first, 3), (second, 6))]
        for r, size, value in rows:
            da[k, pl.ds(r, size), :] = -(has_left * cs(0, r, size)) * value
        rows = [(r, size, msg("left", 3 + k, r, size), msg("own left", k, r, size)) for r, size in tiles]
        rows += [(first, 1, end("left", 9 + k), end("own left", 3 + k))]
        for r, size, value, own in rows:
            gain = cs(3, r, size) if k else cs(2, r, size) + 2.0 * cs(3, r, size)
            wa[k, pl.ds(r, size), :] = has_left * (value + gain * (own + da[k, pl.ds(r, size), :]))
        rows = [(r, size, msg("own right", k, r, size), msg("right", k, r, size)) for r, size in tiles]
        rows += [(r, 1, end("own right", at + k), end("right", at + k)) for r, at in ((lowest, 0), (first, 3))]
        for r, size, value, other in rows:
            change = -(has_right * cs(0, r, size)) * value
            db[k, pl.ds(r, size), :] = change
            qb[k, pl.ds(r, size), :] = has_right * other + change

    def strain_of(buf, r, size, ahead=None):
        grads = []
        for i in range(3):
            here = buf[i, pl.ds(r, size), :]
            beyond = -here if ahead is None else ahead[i, pl.ds(r, size), :] - here
            grads.append([beyond, buf[i, pl.ds(r + 1, size), :] - here, fore_lane(here)])
        return grads

    for out, src, ends in ((ds, da, (lowest, first)), (es, db, (lowest,))):
        parts = [(r, size, range(6)) for r, size in tiles]
        parts += [(r, 1, top if r == lowest else range(6)) for r in ends]
        for r, size, wanted in parts:
            terms = stress_terms(strain_of(src, r, size), cs(2, r, size), cs(3, r, size), wanted)
            for c in wanted:
                out[c, pl.ds(r, size), :] = terms[c]

    for r, size in tiles + [(first, 1)]:
        rb, dq = cs(0, r, size), cs(1, r, size)
        for k in range(3):
            a, b, c = pair_table[k]
            here = ds[a, pl.ds(r, size), :]
            total = here - wa[k, pl.ds(r, size), :]
            total = total + (ds[b, pl.ds(r, size), :] - ds[b, pl.ds(r - 1, size), :])
            total = total + back_lane(ds[c, pl.ds(r, size), :])
            dv[k, pl.ds(r, size), :] = dq * da[k, pl.ds(r, size), :] + rb * total
            dw[k, pl.ds(r, size), :] = -rb * here

    def last_stress(c, r, size):
        q = qb[0 if c < 3 else c - 2, pl.ds(r, size), :]
        if c == 0:
            return (cs(2, r, size) + 2.0 * cs(3, r, size)) * q
        return (cs(2, r, size) if c < 3 else cs(3, r, size)) * q

    for r, size in tiles + [(first, 1)]:
        rb, dq = cs(0, r, size), cs(1, r, size)
        full = [last_stress(c, r, size) for c in range(5)]
        totals = [
            full[0] + (full[3] - last_stress(3, r - 1, size)) + back_lane(full[4]),
            full[3] + (full[1] - last_stress(1, r - 1, size)),
            full[4] + back_lane(full[2]),
        ]
        for k in range(3):
            ev[k, pl.ds(r, size), :] = rb * totals[k]
        if r == first:
            continue
        for k in range(3):
            a, b, c = pair_table[k]
            total = es[a, pl.ds(r, size), :] - (msg("own right", 3 + k, r, size) + full[a])
            total = total + (es[b, pl.ds(r, size), :] - es[b, pl.ds(r - 1, size), :])
            total = total + back_lane(es[c, pl.ds(r, size), :])
            change = dq * db[k, pl.ds(r, size), :] + rb * total
            vn[k, pl.ds(r, size), :] = has_right * (msg("right", 3 + k, r, size) + change)

    def put(buf, dst, x, i):
        copy = pltpu.make_async_copy(buf, dst.at[:, x], sems.at[i])
        copy.start()
        return copy

    copies = []
    for buf, x, change in ((v0.at[:, 0], 0, dv), (v0.at[:, 1], 1, dw), (v1.at[:, 0], n - 1, ev)):
        for r, size in tiles:
            out, at = pl.ds(r - PAD, size), pl.ds(r, size)
            for k in range(3):
                buf[k, out, :] = vb[k, x + 1, at, :] + change[k, at, :]
        copies.append(put(buf, v_out, x, len(copies)))
    for buf, x, src, ahead, more in (
        (s0.at[:, 0], 0, dv, dw, lambda c, r: ds[c, pl.ds(r, 8), :]),
        (s0.at[:, 1], 1, dw, None, None),
        (s1.at[:, 0], n - 1, ev, vn, lambda c, r: None if c == 5 else last_stress(c, r, 8)),
    ):
        for r, size in tiles:
            out, at = pl.ds(r - PAD, size), pl.ds(r, size)
            terms = stress_terms(strain_of(src, r, size, ahead), cs(2, r, size), cs(3, r, size))
            for c in range(6):
                extra = None if more is None else more(c, r)
                term = terms[c] if extra is None else terms[c] + extra
                buf[c, out, :] = sb[c, x + 1, at, :] + term
        copies.append(put(buf, s_out, x, len(copies)))
    for r, size in tiles:
        out, at = pl.ds(r - PAD, size), pl.ds(r, size)
        rl, rm = cs(2, r, size), cs(3, r, size)
        e = [ev[k, at, :] for k in range(3)]
        spread = rl * e[0]
        for c, term in enumerate((spread + 2.0 * rm * e[0], spread, spread, rm * e[1], rm * e[2], None)):
            old = sb[c, n - 1, at, :]
            s1[c, 1, out, :] = old if term is None else old + term
    copies.append(put(s1.at[:, 1], s_out, n - 2, len(copies)))
    for copy in copies:
        copy.wait()


def local(velocity, stress, index, table, split, source_x, source_z, source_y, amplitude):
    _, n, m, y = velocity.shape
    f32, i32 = jnp.float32, jnp.int32
    high = m + 16
    dma = pltpu.SemaphoreType.DMA
    sources = (source_x, source_z, source_y, amplitude)
    held = [pltpu.SMEM(a.shape, a.dtype) for a in sources]
    near = [pltpu.SMEM((a.shape[0] + 1,), a.dtype) for a in sources]
    table = table.T
    materials = [pltpu.SMEM((m,), i32), pltpu.SMEM(table.shape, f32)]

    def shape(*dims):
        return jax.ShapeDtypeStruct(dims, f32)

    def kept(*dims):
        return pltpu.VMEM(dims, f32)

    def outside(*dims):
        return pltpu.HBM(dims, f32)

    def room(mib):
        return pltpu.CompilerParams(vmem_limit_bytes=mib * 1024 * 1024)

    def cost(flops, moved):
        return pl.CostEstimate(flops=flops, bytes_accessed=moved, transcendentals=0)

    padded_v, padded_s = kept(3, n + 2, high, y), kept(6, n + 2, high, y)
    edge_a, edge_b, coef = pl.pallas_call(
        functools.partial(edge_kernel, n, m, y),
        out_shape=[kept(MSG, y)] * 2 + [kept(4, high, y)],
        in_specs=[HBM] * 4,
        out_specs=[VMEM] * 3,
        scratch_shapes=[pltpu.VMEM((9, n + 2, 8, y), f32)] * 2 + materials + [dma((6,))],
        compiler_params=room(EDGE_MIB),
        name="edge_levels",
    )(*[pltpu.with_memory_space_constraint(a, pltpu.HBM) for a in (velocity, stress, index, table)])
    got_a, got_b = swap(edge_a, 2, False), swap(edge_b, 2, True)
    split, edge_a = lax.optimization_barrier((split, edge_a))
    vb, sb, raw, coef = pl.pallas_call(
        functools.partial(load_kernel, n, m, y),
        out_shape=[padded_v, padded_s, kept(3, m, y), kept(4, high, y)],
        in_specs=[VMEM, VMEM, VMEM, SMEM] + [ANY] * 4,
        out_specs=[VMEM] * 4,
        input_output_aliases={2: 3},
        scratch_shapes=[*held, *near, dma((4,))],
        compiler_params=room(LOAD_MIB),
        cost_estimate=cost(60 * n * m * y, 4 * 9 * n * m * y),
        name="load_block",
    )(*[pltpu.with_memory_space_constraint(a, pltpu.VMEM) for a in (velocity, stress)], coef, split, *sources)
    plane_a, plane_b, vb, sb, coef = pl.pallas_call(
        functools.partial(plane_kernel, n, m, y),
        out_shape=[kept(6 * m + 16, y)] * 2 + [padded_v, padded_s, kept(4, high, y)],
        in_specs=[VMEM] * 8,
        out_specs=[VMEM] * 5,
        input_output_aliases={4: 2, 5: 3, 7: 4},
        scratch_shapes=[pltpu.VMEM((MSG, y), f32)] * 2,
        compiler_params=room(SMALL_MIB),
        name="edge_planes",
    )(got_a, got_b, edge_a, edge_b, vb, sb, raw, coef)
    next_b = swap(plane_b, 1, True)
    next_a = swap(plane_a, 1, False)
    vb, sb, v_own, s_own = pl.pallas_call(
        functools.partial(rest_kernel, n, m, y),
        out_shape=[padded_v, padded_s, outside(*velocity.shape), outside(*stress.shape)],
        in_specs=[VMEM] * 3 + [ANY] * 4,
        out_specs=[VMEM, VMEM, HBM, HBM],
        input_output_aliases={0: 0, 1: 1},
        scratch_shapes=[*held, *near, dma((4,)), dma((2, n))],
        compiler_params=room(SMALL_MIB),
        cost_estimate=cost(60 * n * m * y, 4 * 9 * n * m * y),
        name="both_steps",
    )(vb, sb, coef, *sources)
    plane = pltpu.VMEM((3, high, y), f32)
    plane6 = pltpu.VMEM((6, high, y), f32)
    return pl.pallas_call(
        functools.partial(join_kernel, n, m, y),
        out_shape=[outside(*velocity.shape), outside(*stress.shape)],
        in_specs=[VMEM] * 7 + [HBM] * 2,
        out_specs=[HBM, HBM],
        input_output_aliases={7: 0, 8: 1},
        scratch_shapes=[plane, plane, plane6, plane, plane, plane, plane, plane6, plane, plane]
        + [pltpu.VMEM((3, 2, m, y), f32), pltpu.VMEM((3, 1, m, y), f32)]
        + [pltpu.VMEM((6, 2, m, y), f32)] * 2
        + [dma((7,))],
        compiler_params=room(SMALL_MIB),
        name="join_neighbours",
    )(next_b, next_a, plane_a, plane_b, coef, vb, sb, v_own, s_own)


def solution(mesh):
    block = P("member", "horiz", "vert", None)
    return jax.shard_map(
        local,
        mesh=mesh,
        in_specs=(block, block, P("vert"), P(), P(), P(), P(), P(), P("member")),
        out_specs=(block, block),
        check_vma=False,
    )
```
